32 devices in a mesh: group: 4 (over y, x), lat: 4 (over z), lon: 2 (over core).
Axes of the slice: x: 2, y: 2, z: 4, core: 2. Of those that a mesh axis runs over, the one named last changes fastest.
Arguments:
- species_amounts: float32 [128, 4, 64, 256], P('group', None, 'lat', 'lon'), may hold values from -4 to 4
- zonal_cell_fraction: float32 [4, 64, 256], P('group', 'lat', 'lon'), may hold values from -0.3 to 0.3
- meridional_cell_fraction: float32 [4, 64, 256], P('group', 'lat', 'lon'), may hold values from -0.3 to 0.3
- updraft_cell_fraction: float32 [4, 64, 256], P('group', 'lat', 'lon'), may hold values from -0.3 to 0.3
- warmth_anomaly: float32 [4, 64, 256], P('group', 'lat', 'lon'), may hold values from -2 to 2
- mass_per_volume: float32 [4, 64, 256], P('group', 'lat', 'lon'), may hold values from 0.5 to 2
- chemistry_iterations: int32 [64, 256], P('lat', 'lon'), may hold values from 1 to 2, as said below
- companion_species: bfloat16 [512, 128], replicated, may hold values from -0.5 to 0.5
- stoichiometric_rate: bfloat16 [128, 512], replicated, may hold values from -0.25 to 0.25
- heat_yield: float32 [128], replicated, may hold values from -0.5 to 0.5
Outputs:
- tracers_out: float32 [128, 4, 64, 256], P('group', None, 'lat', 'lon')
- east_out: float32 [4, 64, 256], P('group', 'lat', 'lon')
- north_out: float32 [4, 64, 256], P('group', 'lat', 'lon')
- temp_out: float32 [4, 64, 256], P('group', 'lat', 'lon')
The draws below stay inside these ranges and needn't reach their ends.
Inputs may be any that keep to these rules, and one draw needn't show every extreme that they name: `chemistry_iterations`: columns at latitude rows 48 and above hold 1 or 2, and the last row holds 2; all other columns hold 1.
All inputs are finite; a program needn't handle non-finite values.
Results may differ from the reference program's by a relative error of at most 0.0011.
Values sent between devices are 32-bit elements; how exact they have to be, the bound alone decides.
No kernel may reach another device: no remote copies, remote signals or barrier semaphores. Data moves between devices by JAX's collectives and lax.ppermute only.
A program may use at most 64 MiB of HBM per device.

```python
import jax
import jax.numpy as jnp
from jax import lax

NTR = 128
NRX = 512
MAXSUB = 2
STEPS = 1
STRATUM_TOTAL = 4
MERIDIAN_SPAN = 64
PARALLEL_SPAN = 256


def draw_chemistry_iterations(key, part):
    meridian_span = lax.broadcasted_iota(jnp.int32, (MERIDIAN_SPAN, PARALLEL_SPAN), 0)
    jitter = jax.random.randint(key, (MERIDIAN_SPAN, PARALLEL_SPAN), 0, 2).astype(jnp.int32)
    sunlit = meridian_span >= 3 * MERIDIAN_SPAN // 4
    not_last = (meridian_span != MERIDIAN_SPAN - 1).astype(jnp.int32)
    bright = MAXSUB - jitter * not_last
    return jnp.where(sunlit, bright, jnp.ones_like(bright)).astype(jnp.int32)


def levels(key, extent, split, least, largest):
    loudness = 1.0
    for axis_at, blocks in split:
        steps = jax.random.uniform(jax.random.fold_in(jax.random.fold_in(key, 6), axis_at), (blocks,), jnp.float32, least / len(split), largest / len(split))
        loudness = loudness * jnp.repeat(jnp.exp(steps), extent[axis_at] // blocks).reshape((-1,) + (1,) * (len(extent) - 1 - axis_at))
    return loudness


def gaussian(rng, shape, spread, most, cuts=(), dtype=jnp.bfloat16):
    values = spread * jax.random.normal(rng, shape, jnp.float32)
    if cuts:
        values = values * levels(rng, shape, cuts, -0.22, 0.18)
    return jnp.clip(values, -most, most).astype(dtype)


def setup_inputs(seed: int = 0) -> dict:
    key_list = jax.random.split(jax.random.key(seed), 11)
    species_amounts = gaussian(key_list[0], (NTR, STRATUM_TOTAL, MERIDIAN_SPAN, PARALLEL_SPAN), 1.0, 4.0, ((0, 4), (2, 4), (3, 2)), jnp.float32)
    zonal_cell_fraction = jnp.clip(jax.random.uniform(key_list[1], (STRATUM_TOTAL, MERIDIAN_SPAN, PARALLEL_SPAN), jnp.float32, -0.3, 0.3) * levels(key_list[1], (STRATUM_TOTAL, MERIDIAN_SPAN, PARALLEL_SPAN), ((0, 4), (1, 4), (2, 2)), -0.4, 0.0), -0.3, 0.3)
    meridional_cell_fraction = jnp.clip(jax.random.uniform(key_list[2], (STRATUM_TOTAL, MERIDIAN_SPAN, PARALLEL_SPAN), jnp.float32, -0.3, 0.3) * levels(key_list[2], (STRATUM_TOTAL, MERIDIAN_SPAN, PARALLEL_SPAN), ((0, 4), (1, 4), (2, 2)), -0.4, 0.0), -0.3, 0.3)
    updraft_cell_fraction = jnp.clip(jax.random.uniform(key_list[3], (STRATUM_TOTAL, MERIDIAN_SPAN, PARALLEL_SPAN), jnp.float32, -0.3, 0.3) * levels(key_list[3], (STRATUM_TOTAL, MERIDIAN_SPAN, PARALLEL_SPAN), ((0, 4), (1, 4), (2, 2)), -0.4, 0.0), -0.3, 0.3)
    warmth_anomaly = gaussian(key_list[4], (STRATUM_TOTAL, MERIDIAN_SPAN, PARALLEL_SPAN), 0.5, 2.0, ((0, 4), (1, 4), (2, 2)), jnp.float32)
    mass_per_volume = jnp.clip(0.5 + 1.5 * jax.random.uniform(key_list[5], (STRATUM_TOTAL, MERIDIAN_SPAN, PARALLEL_SPAN), jnp.float32) ** levels(key_list[5], (STRATUM_TOTAL, MERIDIAN_SPAN, PARALLEL_SPAN), ((0, 4), (1, 4), (2, 2)), -0.2, 0.2), 0.5, 2.0)
    chemistry_iterations = draw_chemistry_iterations(jax.random.fold_in(key_list[10], 71), 0)
    companion_species = gaussian(key_list[7], (NRX, NTR), NTR ** -0.5, 0.5)
    stoichiometric_rate = gaussian(key_list[8], (NTR, NRX), NRX ** -0.5, 0.25)
    heat_yield = gaussian(key_list[9], (NTR,), NTR ** -0.5, 0.5, (), jnp.float32)
    return dict(species_amounts=species_amounts, zonal_cell_fraction=zonal_cell_fraction, meridional_cell_fraction=meridional_cell_fraction, updraft_cell_fraction=updraft_cell_fraction, warmth_anomaly=warmth_anomaly, mass_per_volume=mass_per_volume, chemistry_iterations=chemistry_iterations, companion_species=companion_species, stoichiometric_rate=stoichiometric_rate, heat_yield=heat_yield)


diffusion = 0.1
pressure = 0.05
chem_step = 0.2
block_cells = 512


def transport(padded, east_pad, north_pad, upward):
    zonal_cells = padded[..., 1:-1, :]
    zonal_wind = east_pad[:, 1:-1, :]
    face_wind = 0.5 * (zonal_wind[..., :-1] + zonal_wind[..., 1:])
    face_flux = jnp.maximum(face_wind, 0.0) * zonal_cells[..., :-1] + jnp.minimum(face_wind, 0.0) * zonal_cells[..., 1:]
    change = face_flux[..., 1:] - face_flux[..., :-1]
    north_cells = padded[..., 1:-1]
    north_wind = north_pad[:, :, 1:-1]
    face_wind = 0.5 * (north_wind[:, :-1] + north_wind[:, 1:])
    face_flux = jnp.maximum(face_wind, 0.0) * north_cells[..., :-1, :] + jnp.minimum(face_wind, 0.0) * north_cells[..., 1:, :]
    change = change + (face_flux[..., 1:, :] - face_flux[..., :-1, :])
    centre = padded[..., 1:-1, 1:-1]
    face_wind = 0.5 * (upward[:-1] + upward[1:])
    face_flux = jnp.maximum(face_wind, 0.0) * centre[..., :-1, :, :] + jnp.minimum(face_wind, 0.0) * centre[..., 1:, :, :]
    closed = jnp.zeros_like(face_flux[..., :1, :, :])
    face_flux = jnp.concatenate([closed, face_flux, closed], axis=-3)
    change = change + (face_flux[..., 1:, :, :] - face_flux[..., :-1, :, :])
    return centre - change


def dynamics(padded):
    centre = padded[:, :, 1:-1, 1:-1]
    eastern = padded[:, :, 1:-1, 2:]
    western = padded[:, :, 1:-1, :-2]
    northern = padded[:, :, 2:, 1:-1]
    southern = padded[:, :, :-2, 1:-1]
    laplace = eastern + western + northern + southern - 4.0 * centre
    diffused = centre + diffusion * laplace
    zonal_axis_name = diffused[0] - pressure * (eastern[2] - western[2])
    meridional_axis_name = diffused[1] - pressure * (northern[2] - southern[2])
    return zonal_axis_name, meridional_axis_name, diffused[2]


def react_block(tracer_block, rate_block, count_block, companion_species, stoichiometric_rate, heat_yield):
    species = tracer_block.shape[0]
    width = tracer_block.shape[1]
    repeats = companion_species.shape[0] // species
    deepest = jnp.max(count_block)

    def keep_going(state_pair):
        return state_pair[0] < deepest

    def substep(state_pair):
        counter, current = state_pair
        narrow = current.astype(jnp.bfloat16)
        pair_terms = jnp.dot(companion_species, narrow, preferred_element_type=jnp.float32)
        quadratic = (pair_terms.reshape(repeats, species, width) * current[None]).reshape(repeats * species, width).astype(jnp.bfloat16)
        tendency = rate_block[None] * jnp.dot(stoichiometric_rate, quadratic, preferred_element_type=jnp.float32) - current
        current = jnp.where(counter < count_block[None], current + chem_step * tendency, current)
        return counter + 1, current

    final = lax.while_loop(keep_going, substep, (jnp.zeros((), jnp.int32), tracer_block))[1]
    heating = jnp.dot(heat_yield[None], final - tracer_block, precision=lax.Precision.HIGHEST)[0]
    return final, heating


def reference(species_amounts, zonal_cell_fraction, meridional_cell_fraction, updraft_cell_fraction, warmth_anomaly, mass_per_volume, chemistry_iterations, companion_species, stoichiometric_rate, heat_yield):
    species = species_amounts.shape[0]
    stratum_total, meridian_span, parallel_span = warmth_anomaly.shape
    cell_count = stratum_total * meridian_span * parallel_span
    block_count = cell_count // block_cells
    counts = jnp.broadcast_to(chemistry_iterations[None], (stratum_total, meridian_span, parallel_span)).reshape(block_count, block_cells).astype(jnp.int32)
    zonal_axis_name, meridional_axis_name, heat_snapshot = zonal_cell_fraction, meridional_cell_fraction, warmth_anomaly
    concentration = species_amounts
    for coupling in range(STEPS):
        fields = jnp.stack([zonal_axis_name, meridional_axis_name, heat_snapshot])
        padded_fields = jnp.pad(fields, ((0, 0), (0, 0), (1, 1), (1, 1)))
        padded_tracers = jnp.pad(concentration, ((0, 0), (0, 0), (1, 1), (1, 1)))
        advected = transport(padded_tracers, padded_fields[0], padded_fields[1], updraft_cell_fraction)
        new_east, new_north, warmed = dynamics(padded_fields)
        reaction_rate = jax.nn.sigmoid(2.0 * heat_snapshot).reshape(block_count, block_cells)
        blocks = advected.reshape(species, block_count, block_cells).transpose(1, 0, 2)

        def one_block(pieces):
            return react_block(pieces[0], pieces[1], pieces[2], companion_species, stoichiometric_rate, heat_yield)

        reacted, heating = lax.map(one_block, (blocks, reaction_rate, counts))
        concentration = reacted.transpose(1, 0, 2).reshape(concentration.shape)
        heat_snapshot = warmed + heating.reshape(stratum_total, meridian_span, parallel_span) / mass_per_volume
        zonal_axis_name, meridional_axis_name = new_east, new_north
    return concentration, zonal_axis_name, meridional_axis_name, heat_snapshot
```

```python
import functools

import jax
import jax.numpy as jnp
from jax import lax
from jax.experimental import pallas as pl
from jax.experimental.pallas import tpu as pltpu
from jax.sharding import PartitionSpec as P

diffusion = 0.1
pressure = 0.05
chem_step = 0.2

VMEM = pl.BlockSpec(memory_space=pltpu.VMEM)
SMEM = pl.BlockSpec(memory_space=pltpu.SMEM)
F32 = jnp.float32


def struct(*shape, dtype=F32):
    return jax.ShapeDtypeStruct(shape, dtype)


def call(kernel, out_shape, n_in, flops=0, touched=0, scratch=()):
    return pl.pallas_call(
        kernel,
        out_shape=out_shape,
        in_specs=[SMEM] + [VMEM] * (n_in - 1),
        out_specs=jax.tree.map(lambda _: VMEM, out_shape),
        scratch_shapes=list(scratch),
        compiler_params=pltpu.CompilerParams(vmem_limit_bytes=40 * 1024 * 1024),
        cost_estimate=pl.CostEstimate(flops=flops, bytes_accessed=touched, transcendentals=0),
    )


def even_pairs(count):
    return [(i, i ^ 1) for i in range(count) if (i ^ 1) < count]


def odd_pairs(count):
    pairs = []
    for i in range(1, count - 1, 2):
        pairs += [(i, i + 1), (i + 1, i)]
    return pairs


def neighbours(messages, axis):
    count = lax.axis_size(axis)
    return [
        lax.ppermute(m, axis, pairs)
        for m, pairs in zip(messages, (even_pairs(count), odd_pairs(count)))
    ]


def partner_swap(block, hop):
    return lax.ppermute(block, "group", [(i, i ^ hop) for i in range(lax.axis_size("group"))])


def lane_ids(shape):
    return lax.broadcasted_iota(jnp.int32, shape, len(shape) - 1)


def row_ids(shape):
    return lax.broadcasted_iota(jnp.int32, shape, len(shape) - 2)


def pack_columns(ids, species, east, north, warmth, *messages):
    tracers, strata, rows, width = species.shape
    lane = lane_ids((rows, width))
    for at, message in enumerate(messages):
        high = ids[2] == at
        edge = jnp.where(high, width - 1, 0)

        def one(t, acc):
            for k in range(strata):
                place = t * strata + k
                turned = pltpu.roll(species[t, k], lax.rem(place - edge + width, width), 1)
                acc = jnp.where(lane == place, turned, acc)
            return acc

        message[0:rows] = lax.fori_loop(0, tracers, one, jnp.zeros((rows, width), F32), unroll=4)
        fields = jnp.zeros((rows, width), F32)
        for place, field in enumerate((east, north, warmth)):
            turned = pltpu.roll(field[0], lax.rem(place - edge + width, width), 1)
            fields = jnp.where(lane == place, turned, fields)
        message[rows:2 * rows] = fields


def middle(value):
    quarter = value.shape[0] // 4
    return value[quarter:3 * quarter]


def rims(value):
    quarter = value.shape[0] // 4
    return jnp.concatenate([value[:quarter], value[3 * quarter:]], axis=0)


def faces(low, high):
    wind = 0.5 * (low + high)
    return jnp.maximum(wind, 0.0), jnp.minimum(wind, 0.0)


def rim_lanes(even, got, place):
    columns = [g[:, place:place + 1] for g in got]
    if len(columns) == 1:
        columns.append(jnp.zeros_like(columns[0]))
    return (
        jnp.where(even, columns[1], columns[0]),
        jnp.where(even, columns[0], columns[1]),
    )


def transport_kernel(chunk, n_lon, n_lat, slots, ids, species, *refs):
    refs = list(refs)
    winds = [refs.pop(0) for _ in range(slots)]
    lon_in = [refs.pop(0) for _ in range(n_lon)]
    lat_in = [refs.pop(0) for _ in range(n_lat)] if chunk else []
    outs = [refs.pop(0) for _ in range(slots)]
    lat_out = [] if chunk else [refs.pop(0) for _ in range(n_lat)]
    upward = refs.pop(0)
    tracers, strata, rows, width = species.shape
    half = rows // 2
    quarter = rows // 4
    me, lat_even, lon_even = ids[0], ids[1] == 0, ids[2] == 0
    pick = rims if chunk else middle
    lane = lane_ids((half, width))
    row = row_ids((half, width))
    whole_lane = lane_ids((rows, width))
    whole_row = row_ids((rows, width))

    for slot in range(slots):
        upward[me ^ slot] = winds[slot][2]

    def north_rims(level):
        if not chunk:
            zero = jnp.zeros((1, width), F32)
            return zero, zero
        got = [m[pl.ds(tracers * strata + level, 1), :] for m in lat_in]
        if len(got) == 1:
            got.append(jnp.zeros_like(got[0]))
        return jnp.where(lat_even, got[1], got[0]), jnp.where(lat_even, got[0], got[1])

    coefficients = []
    for slot in range(slots):
        level = me ^ slot
        east, north, up = winds[slot][0], winds[slot][1], winds[slot][2]
        low, high = rim_lanes(lon_even, [winds[slot][3 + at] for at in range(n_lon)], 0)
        east_next = jnp.where(whole_lane == width - 1, high, pltpu.roll(east, width - 1, 1))
        east_last = jnp.where(whole_lane == 0, low, pltpu.roll(east, 1, 1))
        low, high = north_rims(level)
        north_next = jnp.where(whole_row == rows - 1, high, pltpu.roll(north, rows - 1, 0))
        north_last = jnp.where(whole_row == 0, low, pltpu.roll(north, 1, 0))
        above = upward[jnp.minimum(level + 1, strata - 1)]
        below = upward[jnp.maximum(level - 1, 0)]
        has_above = jnp.where(level < strata - 1, 1.0, 0.0)
        has_below = jnp.where(level > 0, 1.0, 0.0)
        east_out, east_in = faces(east, east_next)
        west_in, west_out = faces(east_last, east)
        north_out, north_in = faces(north, north_next)
        south_in, south_out = faces(north_last, north)
        up_out, up_in = [has_above * f for f in faces(up, above)]
        down_in, down_out = [has_below * f for f in faces(below, up)]
        stay = 1.0 - (
            (east_out - west_out) + (north_out - south_out) + (up_out - down_out)
        )
        coefficients.append(
            [pick(f) for f in (stay, -east_in, west_in, -north_in, south_in, -up_in, down_in)]
        )

    columns = [pick(m[0:rows]) for m in lon_in]
    if n_lon == 2:
        columns = [jnp.where(lon_even, columns[1], columns[0]), jnp.where(lon_even, columns[0], columns[1])]
    else:
        missing = jnp.where(lon_even, 0, width - 1)
        for c in coefficients:
            at = 2 if False else None
            c[1] = jnp.where((lane == width - 1) & (missing == width - 1), 0.0, c[1])
            c[2] = jnp.where((lane == 0) & (missing == 0), 0.0, c[2])

    def one(t, carry):
        for slot in range(slots):
            level = me ^ slot
            stay, east_in, west_in, north_in, south_in, up_in, down_in = coefficients[slot]
            place = t * strata + level
            if n_lon == 2:
                low = pltpu.roll(columns[0], lax.rem(width - place, width), 1)
                high = pltpu.roll(columns[1], width - 1 - place, 1)
            else:
                edge = jnp.where(lon_even, width - 1, 0)
                low = high = pltpu.roll(columns[0], lax.rem(width + edge - place, width), 1)
            above = jnp.minimum(level + 1, strata - 1)
            below = jnp.maximum(level - 1, 0)
            if chunk:
                first, last = species[t, level, 0:half], species[t, level, half:rows]
                here = jnp.where(row < quarter, first, last)
                got = [m[pl.ds(place, 1), :] for m in lat_in]
                if len(got) == 1:
                    got.append(jnp.zeros_like(got[0]))
                south_rim = jnp.where(lat_even, got[1], got[0])
                north_rim = jnp.where(lat_even, got[0], got[1])
                south = jnp.where(row < quarter - 1, first, last)
                south = jnp.where(row == 0, south_rim, pltpu.roll(south, 1, 0))
                north = jnp.where(row < quarter + 1, first, last)
                north = jnp.where(row == half - 1, north_rim, pltpu.roll(north, half - 1, 0))
                up = jnp.where(row < quarter, species[t, above, 0:half], species[t, above, half:rows])
                down = jnp.where(row < quarter, species[t, below, 0:half], species[t, below, half:rows])
            else:
                here = species[t, level, quarter:3 * quarter]
                south = species[t, level, quarter - 1:3 * quarter - 1]
                north = species[t, level, quarter + 1:3 * quarter + 1]
                up = species[t, above, quarter:3 * quarter]
                down = species[t, below, quarter:3 * quarter]
            east = jnp.where(lane == width - 1, high, pltpu.roll(here, width - 1, 1))
            west = jnp.where(lane == 0, low, pltpu.roll(here, 1, 1))
            value = (
                (stay * here + east_in * east)
                + (west_in * west + north_in * north)
                + (south_in * south + up_in * up)
                + down_in * down
            )
            outs[slot][pl.ds(t, half, stride=tracers), :] = value
        return carry

    lax.fori_loop(0, tracers, one, 0, unroll=2)

    for at, message in enumerate(lat_out):
        top = ids[1] == at
        edge = jnp.where(top, rows - 1, 0)

        def pack(t, carry):
            block = [species[t, k, pl.ds(edge, 1), :] for k in range(strata)]
            for k in range(strata):
                message[pl.ds(t * strata + k, 1), :] = block[k]
            return carry

        lax.fori_loop(0, tracers, pack, 0, unroll=4)
        base = tracers * strata
        for slot in range(slots):
            message[pl.ds(base + (me ^ slot), 1), :] = winds[slot][1, pl.ds(edge, 1), :]
        message[base + strata:base + strata + 1] = winds[0][0, pl.ds(edge, 1), :]
        message[base + strata + 1:base + strata + 2] = winds[0][3 + n_lon, pl.ds(edge, 1), :]


def chemistry_kernel(chunk, slots, ids, deepest, *refs):
    refs = list(refs)
    advected = [refs.pop(0) for _ in range(slots)]
    warmth, counts, companion, stoichiometry, yields = [refs.pop(0) for _ in range(5)]
    outs = [refs.pop(0) for _ in range(slots)]
    heat = refs.pop(0)
    current = refs.pop(0)
    start = refs.pop(0)
    half, owned, width = advected[0].shape
    species = slots * owned
    repeats = companion.shape[0] // species
    me = ids[0]
    pick = rims if chunk else middle
    for slot in range(slots):
        first = pl.multiple_of((me ^ slot) * owned, owned)
        current[:, pl.ds(first, owned), :] = advected[slot][...]
        start[:, pl.ds(first, owned), :] = advected[slot][...]
    rate = jax.nn.sigmoid(2.0 * pick(warmth[0]))
    many = pick(counts[...])
    pair = 2

    def substep(s, carry):
        for r in range(0, half, pair):
            now = jnp.concatenate([current[r + p] for p in range(pair)], axis=1)
            pairs = jnp.dot(companion[...], now.astype(jnp.bfloat16), preferred_element_type=F32)
            quad = (pairs.reshape(repeats, species, pair * width) * now[None]).astype(jnp.bfloat16)
            made = jnp.dot(
                stoichiometry[...],
                quad.reshape(repeats * species, pair * width),
                preferred_element_type=F32,
            )
            row_rate = jnp.concatenate([rate[r + p:r + p + 1] for p in range(pair)], axis=1)
            row_many = jnp.concatenate([many[r + p:r + p + 1] for p in range(pair)], axis=1)
            after = now + chem_step * (row_rate * made - now)
            after = jnp.where(s < row_many, after, now)
            for p in range(pair):
                current[r + p] = after[:, p * width:(p + 1) * width]
        return carry

    lax.fori_loop(0, deepest[0], substep, 0)
    weight = jnp.broadcast_to(yields[...], (species, species)).T[:, 0:1]
    for r in range(half):
        heat[r:r + 1] = jnp.sum(weight * (current[r] - start[r]), axis=0, keepdims=True)
    for slot in range(slots):
        first = pl.multiple_of((me ^ slot) * owned, owned)
        outs[slot][...] = current[:, pl.ds(first, owned), :]


def dynamics_kernel(n_lon, n_lat, base, strata, ids, fields, *refs):
    refs = list(refs)
    lon_in = [refs.pop(0) for _ in range(n_lon)]
    lat_in = [refs.pop(0) for _ in range(n_lat)]
    east_out, north_out, warmed = refs
    rows, width = warmed.shape[1:]
    me, lat_even, lon_even = ids[0], ids[1] == 0, ids[2] == 0
    lane = lane_ids((rows, width))
    row = row_ids((rows, width))

    def around(value, place, rim_row):
        low, high = rim_lanes(lon_even, [m[rows:2 * rows] for m in lon_in], place)
        east = jnp.where(lane == width - 1, high, pltpu.roll(value, width - 1, 1))
        west = jnp.where(lane == 0, low, pltpu.roll(value, 1, 1))
        got = [m[pl.ds(rim_row, 1), :] for m in lat_in]
        if len(got) == 1:
            got.append(jnp.zeros_like(got[0]))
        low, high = jnp.where(lat_even, got[1], got[0]), jnp.where(lat_even, got[0], got[1])
        north = jnp.where(row == rows - 1, high, pltpu.roll(value, rows - 1, 0))
        south = jnp.where(row == 0, low, pltpu.roll(value, 1, 0))
        laplace = east + west + north + south - 4.0 * value
        return value + diffusion * laplace, east - west, north - south

    east, _, _ = around(fields[0], 0, base + strata)
    north, _, _ = around(fields[1], 1, base + me)
    heat, zonal, meridional = around(fields[3 + n_lon], 2, base + strata + 1)
    east_out[0] = east - pressure * zonal
    north_out[0] = north - pressure * meridional
    warmed[0] = heat


def result_kernel(slots, ids, *refs):
    refs = list(refs)
    centre = [refs.pop(0) for _ in range(slots)]
    edges = [refs.pop(0) for _ in range(slots)]
    heat_centre, heat_edges, warmed, density, out, temp = refs
    tracers, strata, rows, width = out.shape
    half, quarter = rows // 2, rows // 4
    me = ids[0]

    def one(t, carry):
        for slot in range(slots):
            level = me ^ slot
            mid = centre[slot][pl.ds(t, half, stride=tracers), :]
            rim = edges[slot][pl.ds(t, half, stride=tracers), :]
            out[t, level, quarter:3 * quarter] = mid
            out[t, level, 0:quarter] = rim[:quarter]
            out[t, level, 3 * quarter:rows] = rim[quarter:]
        return carry

    lax.fori_loop(0, tracers, one, 0, unroll=2)
    rim = heat_edges[...]
    heating = jnp.concatenate([rim[:quarter], heat_centre[...], rim[quarter:]], axis=0)
    temp[0] = warmed[0] + heating / density[0]


def local(
    species_amounts,
    zonal_cell_fraction,
    meridional_cell_fraction,
    updraft_cell_fraction,
    warmth_anomaly,
    mass_per_volume,
    chemistry_iterations,
    companion_species,
    stoichiometric_rate,
    heat_yield,
):
    slots = lax.axis_size("group")
    n_lat = min(2, lax.axis_size("lat") - 1)
    n_lon = min(2, lax.axis_size("lon") - 1)
    tracers, strata, rows, width = species_amounts.shape
    half = rows // 2
    base = tracers * strata
    ids = jnp.stack(
        [
            lax.axis_index("group"),
            lax.rem(lax.axis_index("lat"), 2),
            lax.rem(lax.axis_index("lon"), 2),
        ]
    ).astype(jnp.int32)
    deepest = jnp.max(chemistry_iterations).reshape(1)

    lon_out = call(
        pack_columns,
        [struct(2 * rows, width)] * n_lon,
        5,
        touched=4 * species_amounts.size,
    )(ids, species_amounts, zonal_cell_fraction, meridional_cell_fraction, warmth_anomaly)
    lon_in = neighbours(lon_out, "lon")
    fields = jnp.concatenate(
        [zonal_cell_fraction, meridional_cell_fraction, updraft_cell_fraction]
        + [m[rows:][None] for m in lon_in]
        + [warmth_anomaly],
        axis=0,
    )
    payload = fields[:3 + n_lon]
    winds = [fields] + [partner_swap(payload, hop) for hop in range(slots - 1, 0, -1)][::-1]

    def transport(chunk, lat_in):
        out_shape = [struct(half * tracers, width)] * slots
        if not chunk:
            out_shape = out_shape + [struct(base + strata + 4, width)] * n_lat
        got = call(
            functools.partial(transport_kernel, chunk, n_lon, n_lat, slots),
            out_shape,
            2 + slots + n_lon + len(lat_in),
            flops=14 * species_amounts.size // 2,
            touched=8 * species_amounts.size,
            scratch=[pltpu.VMEM((strata, rows, width), F32)],
        )(ids, species_amounts, *winds, *lon_in, *lat_in)
        return got[:slots], got[slots:]

    def swap_slots(blocks):
        swapped = {hop: partner_swap(blocks[hop], hop) for hop in range(slots - 1, 0, -1)}
        return [blocks[0]] + [swapped[hop] for hop in range(1, slots)]

    def chemistry(chunk, advected):
        got = pl.pallas_call(
            functools.partial(chemistry_kernel, chunk, slots),
            out_shape=[struct(half, tracers, width)] * slots + [struct(half, width)],
            in_specs=[SMEM, SMEM] + [VMEM] * (slots + 5),
            out_specs=[VMEM] * (slots + 1),
            scratch_shapes=[pltpu.VMEM((half, slots * tracers, width), F32)] * 2,
            compiler_params=pltpu.CompilerParams(vmem_limit_bytes=40 * 1024 * 1024),
            cost_estimate=pl.CostEstimate(
                flops=4 * half * width * companion_species.size,
                bytes_accessed=8 * species_amounts.size,
                transcendentals=0,
            ),
        )(
            ids,
            deepest,
            *[a.reshape(half, tracers, width) for a in advected],
            warmth_anomaly,
            chemistry_iterations,
            companion_species,
            stoichiometric_rate,
            heat_yield[None],
        )
        return [g.reshape(half * tracers, width) for g in got[:slots]], got[slots]

    adv_mid, lat_out = transport(0, [])
    mid = swap_slots(adv_mid)
    lat_in = neighbours(lat_out, "lat")
    adv_rim, _ = transport(1, lat_in)
    rim = swap_slots(adv_rim)
    east_out, north_out, warmed = call(
        functools.partial(dynamics_kernel, n_lon, n_lat, base, strata),
        [struct(1, rows, width)] * 3,
        2 + n_lon + n_lat,
    )(ids, fields, *lon_in, *lat_in)
    mid, heat_mid = chemistry(0, mid)
    mid = swap_slots(mid)
    rim, heat_rim = chemistry(1, rim)
    rim = swap_slots(rim)
    tracers_out, temp_out = call(
        functools.partial(result_kernel, slots),
        [struct(tracers, strata, rows, width), struct(1, rows, width)],
        1 + 2 * slots + 4,
        touched=8 * species_amounts.size,
    )(ids, *mid, *rim, heat_mid, heat_rim, warmed, mass_per_volume)
    return (tracers_out, east_out, north_out, temp_out)


def solution(mesh):
    return jax.shard_map(
        local,
        mesh=mesh,
        in_specs=(
            P("group", None, "lat", "lon"),
            P("group", "lat", "lon"),
            P("group", "lat", "lon"),
            P("group", "lat", "lon"),
            P("group", "lat", "lon"),
            P("group", "lat", "lon"),
            P("lat", "lon"),
            P(),
            P(),
            P(),
        ),
        out_specs=(
            P("group", None, "lat", "lon"),
            P("group", "lat", "lon"),
            P("group", "lat", "lon"),
            P("group", "lat", "lon"),
        ),
        check_vma=False,
    )
```

```python
import functools

import jax
import jax.numpy as jnp
from jax import lax
from jax.experimental import pallas as pl
from jax.experimental.pallas import tpu as pltpu
from jax.sharding import PartitionSpec as P

diffusion = 0.1
pressure = 0.05
chem_step = 0.2

VMEM = pl.BlockSpec(memory_space=pltpu.VMEM)
SMEM = pl.BlockSpec(memory_space=pltpu.SMEM)
ANY = pl.BlockSpec(memory_space=pl.ANY)
HBM = pl.BlockSpec(memory_space=pltpu.HBM)
LIMIT = 40 * 1024 * 1024
F32 = jnp.float32


def struct(*shape, dtype=F32):
    return jax.ShapeDtypeStruct(shape, dtype)


def call(kernel, out_shape, n_in, flops=0, touched=0, scratch=()):
    return pl.pallas_call(
        kernel,
        out_shape=out_shape,
        in_specs=[SMEM] + [VMEM] * (n_in - 1),
        out_specs=jax.tree.map(lambda _: VMEM, out_shape),
        scratch_shapes=list(scratch),
        compiler_params=pltpu.CompilerParams(vmem_limit_bytes=LIMIT),
        cost_estimate=pl.CostEstimate(flops=flops, bytes_accessed=touched, transcendentals=0),
    )


def even_pairs(count):
    return [(i, i ^ 1) for i in range(count) if (i ^ 1) < count]


def odd_pairs(count):
    pairs = []
    for i in range(1, count - 1, 2):
        pairs += [(i, i + 1), (i + 1, i)]
    return pairs


def neighbours(messages, axis):
    count = lax.axis_size(axis)
    return [
        lax.ppermute(m, axis, pairs)
        for m, pairs in zip(messages, (even_pairs(count), odd_pairs(count)))
    ]


def partner_swap(block, hop):
    return lax.ppermute(block, "group", [(i, i ^ hop) for i in range(lax.axis_size("group"))])


def lane_ids(shape):
    return lax.broadcasted_iota(jnp.int32, shape, len(shape) - 1)


def row_ids(shape):
    return lax.broadcasted_iota(jnp.int32, shape, len(shape) - 2)


def pack_kernel(n_lon, n_lat, ids, species_hbm, *refs):
    *outs, species, sem = refs
    copy = pltpu.make_async_copy(species_hbm, species, sem)
    copy.start()
    tracers, strata, rows, width = species.shape
    lane = lane_ids((rows, width))
    flat = species.reshape(tracers * strata * rows, width)
    base = tracers * strata
    copy.wait()
    for at, message in enumerate(outs[n_lon:n_lon + n_lat]):
        edge = jnp.where(ids[1] == at, rows - 1, 0)
        message[...] = flat[pl.ds(edge, base, stride=rows), :]
    for at, message in enumerate(outs[:n_lon]):
        edge = jnp.where(ids[2] == at, width - 1, 0)

        def one(t, acc):
            for k in range(strata):
                place = t * strata + k
                turned = pltpu.roll(species[t, k], lax.rem(place - edge + width, width), 1)
                acc = jnp.where(lane == place, turned, acc)
            return acc

        message[...] = lax.fori_loop(
            0, tracers, one, jnp.zeros((rows, width), F32), unroll=tracers
        )


def both_sides(even, got):
    if len(got) == 1:
        got = [got[0], jnp.zeros_like(got[0])]
    return jnp.where(even, got[1], got[0]), jnp.where(even, got[0], got[1])


def beside(value, even, got):
    width = value.shape[1]
    lane = lane_ids(value.shape)
    low, high = both_sides(even, got)
    west = pltpu.roll(jnp.where(lane == width - 1, low, value), 1, 1)
    east = pltpu.roll(jnp.where(lane == 0, high, value), width - 1, 1)
    return west, east


def beyond(value, even, got):
    rows = value.shape[0]
    row = row_ids(value.shape)
    low, high = both_sides(even, got)
    south = jnp.where(row == 0, low, pltpu.roll(value, 1, 0))
    north = jnp.where(row == rows - 1, high, pltpu.roll(value, rows - 1, 0))
    return south, north


def middle(value):
    quarter = value.shape[0] // 4
    return value[quarter:3 * quarter]


def ends(value):
    quarter = value.shape[0] // 4
    return jnp.concatenate([value[:quarter], value[3 * quarter:]], axis=0)


def faces(low, high):
    wind = 0.5 * (low + high)
    return jnp.maximum(wind, 0.0), jnp.minimum(wind, 0.0)


def transport_kernel(chunk, n_lon, n_lat, slots, ids, species, *refs):
    refs = list(refs)
    winds = [refs.pop(0) for _ in range(slots)]
    lon_in = [refs.pop(0) for _ in range(n_lon)]
    lat_in = [refs.pop(0) for _ in range(n_lat)] if chunk else []
    if chunk:
        counts, yields = refs.pop(0), refs.pop(0)
    outs = [refs.pop(0) for _ in range(slots)]
    if chunk:
        weight, deepest = refs.pop(0), refs.pop(0)
        weight[...] = jnp.broadcast_to(yields[...], weight.shape[::-1]).T
        deepest[0] = jnp.max(counts[...])
    upward = refs.pop(0)
    tracers, strata, rows, width = species.shape
    half = rows // 2
    quarter = rows // 4
    base = tracers * strata
    me, lat_even, lon_even = ids[0], ids[1] == 0, ids[2] == 0
    pick = ends if chunk else middle
    lane = lane_ids((half, width))
    row = row_ids((half, width))
    for slot in range(slots):
        upward[me ^ slot] = winds[slot][2 * rows:3 * rows]

    coefficients = []
    for slot in range(slots):
        level = me ^ slot
        east = winds[slot][0:rows]
        at = (1 + slot) * rows
        east_last, east_next = beside(east, lon_even, [m[at:at + rows] for m in lon_in])
        north = winds[slot][rows:2 * rows]
        rim = [m[base + slot:base + slot + 1] for m in lat_in] or [jnp.zeros((1, width), F32)]
        north_last, north_next = beyond(north, lat_even, rim)
        up = upward[level]
        above = upward[jnp.minimum(level + 1, strata - 1)]
        below = upward[jnp.maximum(level - 1, 0)]
        has_above = jnp.where(level < strata - 1, 1.0, 0.0)
        has_below = jnp.where(level > 0, 1.0, 0.0)
        east_out, east_in = faces(east, east_next)
        west_in, west_out = faces(east_last, east)
        north_out, north_in = faces(north, north_next)
        south_in, south_out = faces(north_last, north)
        up_out, up_in = [has_above * f for f in faces(up, above)]
        down_in, down_out = [has_below * f for f in faces(below, up)]
        stay = 1.0 - (
            (east_out - west_out) + (north_out - south_out) + (up_out - down_out)
        )
        stay, east_in, west_in, north_in, south_in, up_in, down_in = [
            pick(f) for f in (stay, -east_in, west_in, -north_in, south_in, -up_in, down_in)
        ]
        if n_lon < 2:
            east_in = jnp.where((lane == width - 1) & (ids[2] == 1), 0.0, east_in)
            west_in = jnp.where((lane == 0) & (ids[2] == 0), 0.0, west_in)
        coefficients.append((stay, east_in, west_in, north_in, south_in, up_in, down_in))

    columns = [pick(m[0:rows]) for m in lon_in]
    if n_lon == 2:
        columns = both_sides(lon_even, columns)
    edge = jnp.where(lon_even, width - 1, 0)

    def one(t, carry):
        for slot in range(slots):
            level = me ^ slot
            stay, east_in, west_in, north_in, south_in, up_in, down_in = coefficients[slot]
            place = t * strata + level
            if n_lon == 2:
                low = pltpu.roll(columns[0], lax.rem(width - place, width), 1)
                high = pltpu.roll(columns[1], width - 1 - place, 1)
            else:
                low = high = pltpu.roll(columns[0], lax.rem(width + edge - place, width), 1)
            above = jnp.minimum(level + 1, strata - 1)
            below = jnp.maximum(level - 1, 0)
            if chunk:
                first, last = species[t, level, 0:half], species[t, level, half:rows]
                here = jnp.where(row < quarter, first, last)
                low_row, high_row = both_sides(lat_even, [m[pl.ds(place, 1), :] for m in lat_in])
                south = pltpu.roll(jnp.where(row < quarter - 1, first, last), 1, 0)
                south = jnp.where(row == 0, low_row, south)
                north = pltpu.roll(jnp.where(row < quarter + 1, first, last), half - 1, 0)
                north = jnp.where(row == half - 1, high_row, north)
                up = jnp.where(
                    row < quarter, species[t, above, 0:half], species[t, above, half:rows]
                )
                down = jnp.where(
                    row < quarter, species[t, below, 0:half], species[t, below, half:rows]
                )
            else:
                here = species[t, level, quarter:3 * quarter]
                south = species[t, level, quarter - 1:3 * quarter - 1]
                north = species[t, level, quarter + 1:3 * quarter + 1]
                up = species[t, above, quarter:3 * quarter]
                down = species[t, below, quarter:3 * quarter]
            east = jnp.where(lane == width - 1, high, pltpu.roll(here, width - 1, 1))
            west = jnp.where(lane == 0, low, pltpu.roll(here, 1, 1))
            value = (
                (stay * here + east_in * east)
                + (west_in * west + north_in * north)
                + (south_in * south + up_in * up)
                + down_in * down
            )
            outs[slot][pl.ds(t, half, stride=tracers), :] = value
        return carry

    lax.fori_loop(0, tracers, one, 0, unroll=8)


def chemistry_kernel(chunk, slots, ids, deepest, *refs):
    refs = list(refs)
    advected = [refs.pop(0) for _ in range(slots)]
    warmth, counts, companion, stoichiometry, weight = [refs.pop(0) for _ in range(5)]
    outs = [refs.pop(0) for _ in range(slots)]
    heat, current = refs
    half, owned, width = advected[0].shape
    species = slots * owned
    repeats = companion.shape[0] // species
    pick = ends if chunk else middle
    place = [pl.ds(pl.multiple_of((ids[0] ^ slot) * owned, owned), owned) for slot in range(slots)]
    for slot in range(slots):
        current[:, place[slot], :] = advected[slot][...]
    line = lambda field: jnp.concatenate([field[r:r + 1] for r in range(half)], axis=1)
    rate = line(jax.nn.sigmoid(2.0 * pick(warmth[...])))
    many = line(pick(counts[...]))

    def substep(s, carry):
        now = jnp.concatenate([current[r] for r in range(half)], axis=1)
        pairs = jnp.dot(companion[...], now.astype(jnp.bfloat16), preferred_element_type=F32)
        quad = (pairs.reshape(repeats, species, half * width) * now[None]).astype(jnp.bfloat16)
        made = jnp.dot(
            stoichiometry[...],
            quad.reshape(repeats * species, half * width),
            preferred_element_type=F32,
        )
        after = now + chem_step * (rate * made - now)
        after = jnp.where(s < many, after, now)
        for r in range(half):
            current[r] = after[:, r * width:(r + 1) * width]
        return carry

    lax.fori_loop(0, deepest[0], substep, 0)
    total = None
    for slot in range(slots):
        final = current[:, place[slot], :]
        for r in range(half):
            outs[slot][pl.ds(r, owned, stride=half), :] = final[r]
        part = jnp.sum(weight[place[slot], :][None] * (final - advected[slot][...]), axis=1)
        total = part if total is None else total + part
    heat[...] = total


def dynamics_kernel(n_lon, n_lat, base, slots, ids, east, north, warmth, density, *refs):
    refs = list(refs)
    lon_in = [refs.pop(0) for _ in range(n_lon)]
    lat_in = [refs.pop(0) for _ in range(n_lat)]
    heat_middle, heat_ends, east_out, north_out, temp_out = refs
    rows = temp_out.shape[1]
    quarter = rows // 4
    lat_even, lon_even = ids[1] == 0, ids[2] == 0

    def around(value, tile, line):
        west, east = beside(value, lon_even, [m[tile * rows:(tile + 1) * rows] for m in lon_in])
        south, north = beyond(value, lat_even, [m[base + line:base + line + 1] for m in lat_in])
        laplace = east + west + north + south - 4.0 * value
        return value + diffusion * laplace, east - west, north - south

    new_east, _, _ = around(east[0], 1, slots)
    new_north, _, _ = around(north[0], 1 + slots, 0)
    warmed, zonal, meridional = around(warmth[0], 2 + slots, slots + 1)
    heating = jnp.concatenate(
        [heat_ends[:quarter], heat_middle[...], heat_ends[quarter:]], axis=0
    )
    east_out[0] = new_east - pressure * zonal
    north_out[0] = new_north - pressure * meridional
    temp_out[0] = warmed + heating / density[0]


def place_kernel(chunk, slots, ids, *refs):
    got, out, sems = refs[:slots], refs[-2], refs[-1]
    rows = out.shape[2]
    quarter = rows // 4
    starts = (0, 3 * quarter) if chunk else (quarter, 2 * quarter)
    copies = [
        pltpu.make_async_copy(
            got[slot].at[:, part * quarter:(part + 1) * quarter, :],
            out.at[:, ids[0] ^ slot, start:start + quarter, :],
            sems.at[slot, part],
        )
        for slot in range(slots)
        for part, start in enumerate(starts)
    ]
    for copy in copies:
        copy.start()
    for copy in copies:
        copy.wait()


def local(
    species_amounts,
    zonal_cell_fraction,
    meridional_cell_fraction,
    updraft_cell_fraction,
    warmth_anomaly,
    mass_per_volume,
    chemistry_iterations,
    companion_species,
    stoichiometric_rate,
    heat_yield,
):
    slots = lax.axis_size("group")
    n_lat = min(2, lax.axis_size("lat") - 1)
    n_lon = min(2, lax.axis_size("lon") - 1)
    tracers, strata, rows, width = species_amounts.shape
    half = rows // 2
    base = tracers * strata
    ids = jnp.stack(
        [
            lax.axis_index("group"),
            lax.rem(lax.axis_index("lat"), 2),
            lax.rem(lax.axis_index("lon"), 2),
        ]
    ).astype(jnp.int32)

    payload = jnp.concatenate(
        [
            zonal_cell_fraction[0],
            meridional_cell_fraction[0],
            updraft_cell_fraction[0],
            warmth_anomaly[0],
        ],
        axis=0,
    )
    payload = lax.optimization_barrier(payload)
    east, north, warmth = payload[:rows], payload[rows:2 * rows], payload[3 * rows:]
    gathered = {hop: partner_swap(payload, hop) for hop in range(slots - 1, 0, -1)}
    winds = [payload] + [gathered[hop] for hop in range(1, slots)]

    packed = pl.pallas_call(
        functools.partial(pack_kernel, n_lon, n_lat),
        out_shape=[struct(rows, width)] * n_lon
        + [struct(base, width)] * n_lat
        + [struct(tracers, strata, rows, width)],
        in_specs=[SMEM, HBM],
        out_specs=[VMEM] * (n_lon + n_lat + 1),
        scratch_shapes=[pltpu.SemaphoreType.DMA],
        compiler_params=pltpu.CompilerParams(vmem_limit_bytes=52 * 1024 * 1024),
        cost_estimate=pl.CostEstimate(
            flops=species_amounts.size, bytes_accessed=4 * species_amounts.size, transcendentals=0
        ),
    )(ids, species_amounts)
    species = packed[n_lon + n_lat]
    lon_out = [
        jnp.concatenate([m] + [w[:rows] for w in winds] + [north, warmth], axis=0)
        for m in packed[:n_lon]
    ]
    lat_out = []
    for at, m in enumerate(packed[n_lon:n_lon + n_lat]):
        top = ids[1] == at
        lines = [w[rows:2 * rows] for w in winds] + [east, warmth]
        lines = jnp.concatenate([jnp.where(top, f[rows - 1:], f[:1]) for f in lines], axis=0)
        lines = jnp.pad(lines, ((0, -lines.shape[0] % 8), (0, 0)))
        lat_out.append(jnp.concatenate([m, lines], axis=0))
    lon_in = neighbours(lon_out, "lon")
    lat_out, lon_in = lax.optimization_barrier((lat_out, lon_in))
    lat_in = neighbours(lat_out, "lat")

    def transport(chunk, lat_in=()):
        more = [*lat_in, chemistry_iterations, heat_yield[None]] if chunk else []
        return pl.pallas_call(
            functools.partial(transport_kernel, chunk, n_lon, n_lat, slots),
            out_shape=[struct(half * tracers, width)] * slots
            + [struct(slots * tracers, width), struct(1, dtype=jnp.int32)] * chunk,
            in_specs=[SMEM] + [VMEM] * (1 + slots + n_lon + len(more)),
            out_specs=[VMEM] * slots + [VMEM, SMEM] * chunk,
            scratch_shapes=[pltpu.VMEM((strata, rows, width), F32)],
            compiler_params=pltpu.CompilerParams(vmem_limit_bytes=LIMIT),
            cost_estimate=pl.CostEstimate(
                flops=7 * species_amounts.size if chunk else 1,
                bytes_accessed=256 * species_amounts.size if chunk else 1,
                transcendentals=0,
            ),
        )(ids, species, *winds, *lon_in, *more)

    def swap_slots(blocks):
        swapped = {hop: partner_swap(blocks[hop], hop) for hop in range(slots - 1, 0, -1)}
        return [blocks[0]] + [swapped[hop] for hop in range(1, slots)]

    def chemistry(chunk, advected):
        got = pl.pallas_call(
            functools.partial(chemistry_kernel, chunk, slots),
            out_shape=[struct(tracers * half, width)] * slots + [struct(half, width)],
            in_specs=[SMEM, SMEM] + [VMEM] * (slots + 5),
            out_specs=[VMEM] * (slots + 1),
            scratch_shapes=[pltpu.VMEM((half, slots * tracers, width), F32)],
            compiler_params=pltpu.CompilerParams(vmem_limit_bytes=LIMIT),
            cost_estimate=pl.CostEstimate(
                flops=4 * half * width * companion_species.size,
                bytes_accessed=8 * species_amounts.size,
                transcendentals=0,
            ),
        )(
            ids,
            deepest,
            *[a.reshape(half, tracers, width) for a in advected],
            warmth,
            chemistry_iterations,
            companion_species,
            stoichiometric_rate,
            weight,
        )
        return got[:slots], got[slots]

    def put(chunk, blocks, partial):
        return pl.pallas_call(
            functools.partial(place_kernel, chunk, slots),
            out_shape=struct(tracers, strata, rows, width),
            in_specs=[SMEM] + [VMEM] * slots + [ANY] * len(partial),
            out_specs=ANY,
            scratch_shapes=[pltpu.SemaphoreType.DMA((slots, 2))],
            input_output_aliases={1 + slots: 0} if partial else {},
            compiler_params=pltpu.CompilerParams(vmem_limit_bytes=LIMIT),
            cost_estimate=pl.CostEstimate(
                flops=0, bytes_accessed=4 * species_amounts.size, transcendentals=0
            ),
        )(ids, *[b.reshape(tracers, half, width) for b in blocks], *partial)

    mid = list(transport(0))
    mid[1], mid[2], lat_in = lax.optimization_barrier((mid[1], mid[2], lat_in))
    mid = swap_slots(mid)
    *end, weight, deepest = transport(1, lat_in)
    end = swap_slots(end)
    mid, heat_mid = chemistry(0, mid)
    mid = swap_slots(mid)
    end, heat_end = chemistry(1, end)
    end = swap_slots(end)
    east_out, north_out, temp_out = call(
        functools.partial(dynamics_kernel, n_lon, n_lat, base, slots),
        [struct(1, rows, width)] * 3,
        7 + n_lon + n_lat,
    )(
        ids,
        zonal_cell_fraction,
        meridional_cell_fraction,
        warmth_anomaly,
        mass_per_volume,
        *lon_in,
        *lat_in,
        heat_mid,
        heat_end,
    )
    tracers_out = put(1, end, [put(0, mid, [])])
    return (tracers_out, east_out, north_out, temp_out)


def solution(mesh):
    return jax.shard_map(
        local,
        mesh=mesh,
        in_specs=(
            P("group", None, "lat", "lon"),
            P("group", "lat", "lon"),
            P("group", "lat", "lon"),
            P("group", "lat", "lon"),
            P("group", "lat", "lon"),
            P("group", "lat", "lon"),
            P("lat", "lon"),
            P(),
            P(),
            P(),
        ),
        out_specs=(
            P("group", None, "lat", "lon"),
            P("group", "lat", "lon"),
            P("group", "lat", "lon"),
            P("group", "lat", "lon"),
        ),
        check_vma=False,
    )
```

```python
import functools

import jax
import jax.numpy as jnp
from jax import lax
from jax.experimental import pallas as pl
from jax.experimental.pallas import tpu as pltpu
from jax.sharding import PartitionSpec as P

diffusion = 0.1
pressure = 0.05
chem_step = 0.2

VMEM = pl.BlockSpec(memory_space=pltpu.VMEM)
ANY = pl.BlockSpec(memory_space=pl.ANY)
HBM = pl.BlockSpec(memory_space=pltpu.HBM)
LIMIT = 40 * 1024 * 1024
F32 = jnp.float32


def struct(*shape, dtype=F32):
    return jax.ShapeDtypeStruct(shape, dtype)


def call(kernel, out_shape, in_specs, out_specs=None, scratch=(), aliases=None, flops=1, touched=1, limit=LIMIT):
    return pl.pallas_call(
        kernel,
        out_shape=out_shape,
        in_specs=in_specs,
        out_specs=jax.tree.map(lambda _: VMEM, out_shape) if out_specs is None else out_specs,
        scratch_shapes=list(scratch),
        input_output_aliases=aliases or {},
        compiler_params=pltpu.CompilerParams(vmem_limit_bytes=limit),
        cost_estimate=pl.CostEstimate(flops=flops, bytes_accessed=touched, transcendentals=0),
    )


def parity(axis):
    return lax.rem(lax.axis_index(axis), 2)


def even_pairs(count):
    return [(i, i ^ 1) for i in range(count) if (i ^ 1) < count]


def odd_pairs(count):
    pairs = []
    for i in range(1, count - 1, 2):
        pairs += [(i, i + 1), (i + 1, i)]
    return pairs


def neighbours(messages, axis):
    count = lax.axis_size(axis)
    return [
        lax.ppermute(m, axis, pairs)
        for m, pairs in zip(messages, (even_pairs(count), odd_pairs(count)))
    ]


def lat_neighbours(messages):
    rows, columns = lax.axis_size("lat"), lax.axis_size("lon")
    if len(messages) < 2 or rows % 2 or columns % 2:
        return neighbours(messages, "lat")
    partner = dict(odd_pairs(rows))
    pairs = [
        (i * columns + j, partner[i] * columns + j if i in partner else i * columns + (j ^ 1))
        for i in range(rows)
        for j in range(columns)
    ]
    first = lax.ppermute(messages[0], "lat", even_pairs(rows))
    return [first, lax.ppermute(messages[1], ("lat", "lon"), pairs)]


def partner_swap(block, hop):
    return lax.ppermute(block, "group", [(i, i ^ hop) for i in range(lax.axis_size("group"))])


def lane_ids(shape):
    return lax.broadcasted_iota(jnp.int32, shape, len(shape) - 1)


def row_ids(shape):
    return lax.broadcasted_iota(jnp.int32, shape, len(shape) - 2)


def pack_kernel(n_lon, n_lat, parts, species_hbm, *refs):
    *outs, species, sems = refs
    tracers, strata, rows, width = species.shape
    share = tracers // parts
    copies = [
        pltpu.make_async_copy(
            species_hbm.at[pl.ds(part * share, share)],
            species.at[pl.ds(part * share, share)],
            sems.at[part],
        )
        for part in range(parts)
    ]
    for copy in copies:
        copy.start()
    lane = lane_ids((rows, width))
    flat = species.reshape(tracers * strata * rows, width)
    held = share * strata
    columns = [jnp.zeros((rows, width), F32) for _ in range(n_lon)]
    for part, copy in enumerate(copies):
        copy.wait()
        for at, message in enumerate(outs[n_lon:n_lon + n_lat]):
            edge = jnp.where(parity("lat") == at, rows - 1, 0)
            message[part * held:(part + 1) * held] = flat[
                pl.ds(part * held * rows + edge, held, stride=rows), :
            ]
        for at in range(n_lon):
            edge = jnp.where(parity("lon") == at, width - 1, 0)
            for place in range(part * held, (part + 1) * held):
                block = species[place // strata, place % strata]
                turned = pltpu.roll(block, lax.rem(place - edge + width, width), 1)
                columns[at] = jnp.where(lane == place, turned, columns[at])
    for message, block in zip(outs[:n_lon], columns):
        message[...] = block


def both_sides(axis, got):
    even = parity(axis) == 0
    if len(got) == 1:
        got = [got[0], got[0]]
    at = lax.axis_index(axis)
    low = jnp.where(even, got[1], got[0])
    high = jnp.where(even, got[0], got[1])
    return jnp.where(at > 0, low, 0.0), jnp.where(at < lax.axis_size(axis) - 1, high, 0.0)


def beside(value, axis, got):
    width = value.shape[1]
    lane = lane_ids(value.shape)
    low, high = both_sides(axis, got)
    west = pltpu.roll(jnp.where(lane == width - 1, low, value), 1, 1)
    east = pltpu.roll(jnp.where(lane == 0, high, value), width - 1, 1)
    return west, east


def beyond(value, axis, got):
    rows = value.shape[0]
    row = row_ids(value.shape)
    low, high = both_sides(axis, got)
    south = jnp.where(row == 0, low, pltpu.roll(value, 1, 0))
    north = jnp.where(row == rows - 1, high, pltpu.roll(value, rows - 1, 0))
    return south, north


def middle(value):
    quarter = value.shape[0] // 4
    return value[quarter:3 * quarter]


def ends(value):
    quarter = value.shape[0] // 4
    return jnp.concatenate([value[:quarter], value[3 * quarter:]], axis=0)


def faces(low, high):
    wind = 0.5 * (low + high)
    return jnp.maximum(wind, 0.0), jnp.minimum(wind, 0.0)


def transport_kernel(chunk, n_lon, n_lat, slots, species, *refs):
    refs = list(refs)
    winds = [refs.pop(0) for _ in range(slots)]
    lon_in = [refs.pop(0) for _ in range(n_lon)]
    lat_in = [refs.pop(0) for _ in range(n_lat)] if chunk else []
    if chunk:
        yields = refs.pop(0)
    outs = [refs.pop(0) for _ in range(slots)]
    if chunk:
        weight = refs.pop(0)
        weight[...] = jnp.broadcast_to(yields[...], weight.shape[::-1]).T
    upward = refs.pop(0)
    tracers, strata, rows, width = species.shape
    half = rows // 2
    quarter = rows // 4
    base = tracers * strata
    me, lon_even = lax.axis_index("group"), parity("lon") == 0
    pick = ends if chunk else middle
    lane = lane_ids((half, width))
    row = row_ids((half, width))
    for slot in range(slots):
        upward[me ^ slot] = winds[slot][2 * rows:3 * rows]

    coefficients = []
    for slot in range(slots):
        level = me ^ slot
        east = winds[slot][0:rows]
        east_last, east_next = beside(
            east, "lon", [winds[slot][at:at + rows] for at in range(4 * rows, (4 + n_lon) * rows, rows)]
        )
        north = winds[slot][rows:2 * rows]
        rim = [m[base + slot:base + slot + 1] for m in lat_in] or [jnp.zeros((1, width), F32)]
        north_last, north_next = beyond(north, "lat", rim)
        up = upward[level]
        above = upward[jnp.minimum(level + 1, strata - 1)]
        below = upward[jnp.maximum(level - 1, 0)]
        has_above = jnp.where(level < strata - 1, 1.0, 0.0)
        has_below = jnp.where(level > 0, 1.0, 0.0)
        east_out, east_in = faces(east, east_next)
        west_in, west_out = faces(east_last, east)
        north_out, north_in = faces(north, north_next)
        south_in, south_out = faces(north_last, north)
        up_out, up_in = [has_above * f for f in faces(up, above)]
        down_in, down_out = [has_below * f for f in faces(below, up)]
        stay = 1.0 - (
            (east_out - west_out) + (north_out - south_out) + (up_out - down_out)
        )
        stay, east_in, west_in, north_in, south_in, up_in, down_in = [
            pick(f) for f in (stay, -east_in, west_in, -north_in, south_in, -up_in, down_in)
        ]
        if n_lon < 2:
            east_in = jnp.where((lane == width - 1) & ~lon_even, 0.0, east_in)
            west_in = jnp.where((lane == 0) & lon_even, 0.0, west_in)
        coefficients.append((stay, east_in, west_in, north_in, south_in, up_in, down_in))

    columns = [pick(m[0:rows]) for m in lon_in]
    if n_lon == 2:
        columns = both_sides("lon", columns)
    edge = jnp.where(lon_even, width - 1, 0)

    def one(t, carry):
        for slot in range(slots):
            level = me ^ slot
            stay, east_in, west_in, north_in, south_in, up_in, down_in = coefficients[slot]
            place = t * strata + level
            if n_lon == 2:
                low = pltpu.roll(columns[0], lax.rem(width - place, width), 1)
                high = pltpu.roll(columns[1], width - 1 - place, 1)
            else:
                low = high = pltpu.roll(columns[0], lax.rem(width + edge - place, width), 1)
            above = jnp.minimum(level + 1, strata - 1)
            below = jnp.maximum(level - 1, 0)
            if chunk:
                first, last = species[t, level, 0:half], species[t, level, half:rows]
                here = jnp.where(row < quarter, first, last)
                low_row, high_row = both_sides("lat", [m[pl.ds(place, 1), :] for m in lat_in])
                south = pltpu.roll(jnp.where(row < quarter - 1, first, last), 1, 0)
                south = jnp.where(row == 0, low_row, south)
                north = pltpu.roll(jnp.where(row < quarter + 1, first, last), half - 1, 0)
                north = jnp.where(row == half - 1, high_row, north)
                up = jnp.where(
                    row < quarter, species[t, above, 0:half], species[t, above, half:rows]
                )
                down = jnp.where(
                    row < quarter, species[t, below, 0:half], species[t, below, half:rows]
                )
            else:
                here = species[t, level, quarter:3 * quarter]
                south = species[t, level, quarter - 1:3 * quarter - 1]
                north = species[t, level, quarter + 1:3 * quarter + 1]
                up = species[t, above, quarter:3 * quarter]
                down = species[t, below, quarter:3 * quarter]
            east = jnp.where(lane == width - 1, high, pltpu.roll(here, width - 1, 1))
            west = jnp.where(lane == 0, low, pltpu.roll(here, 1, 1))
            value = (
                (stay * here + east_in * east)
                + (west_in * west + north_in * north)
                + (south_in * south + up_in * up)
                + down_in * down
            )
            outs[slot][pl.ds(t, half, stride=tracers), :] = value
        return carry

    lax.fori_loop(0, tracers, one, 0, unroll=8)


def chemistry_kernel(chunk, slots, *refs):
    refs = list(refs)
    advected = [refs.pop(0) for _ in range(slots)]
    warmth, counts, companion, stoichiometry, weight = [refs.pop(0) for _ in range(5)]
    outs = [refs.pop(0) for _ in range(slots)]
    heat, current = refs
    half, owned, width = advected[0].shape
    species = slots * owned
    repeats = companion.shape[0] // species
    pick = ends if chunk else middle
    place = [pl.ds(pl.multiple_of((lax.axis_index("group") ^ slot) * owned, owned), owned) for slot in range(slots)]
    for slot in range(slots):
        current[:, place[slot], :] = advected[slot][...]
    line = lambda field: jnp.concatenate([field[r:r + 1] for r in range(half)], axis=1)
    rate = line(jax.nn.sigmoid(2.0 * pick(warmth[...])))
    many = line(pick(counts[...]))

    def substep(s, carry):
        now = jnp.concatenate([current[r] for r in range(half)], axis=1)
        pairs = jnp.dot(companion[...], now.astype(jnp.bfloat16), preferred_element_type=F32)
        quad = (pairs.reshape(repeats, species, half * width) * now[None]).astype(jnp.bfloat16)
        made = jnp.dot(
            stoichiometry[...],
            quad.reshape(repeats * species, half * width),
            preferred_element_type=F32,
        )
        after = now + chem_step * (rate * made - now)
        after = jnp.where(s < many, after, now)
        for r in range(half):
            current[r] = after[:, r * width:(r + 1) * width]
        return carry

    deepest = jnp.max(many)
    substep(0, 0)
    lax.fori_loop(1, deepest, substep, 0)
    total = None
    for slot in range(slots):
        final = current[:, place[slot], :]
        for r in range(half):
            outs[slot][pl.ds(r, owned, stride=half), :] = final[r]
        part = jnp.sum(weight[place[slot], :][None] * (final - advected[slot][...]), axis=1)
        total = part if total is None else total + part
    heat[...] = total


def dynamics_kernel(n_lon, n_lat, base, slots, east, north, warmth, density, *refs):
    refs = list(refs)
    lon_in = [refs.pop(0) for _ in range(n_lon)]
    lat_in = [refs.pop(0) for _ in range(n_lat)]
    heat_middle, heat_ends, east_out, north_out, temp_out = refs
    rows = temp_out.shape[1]
    quarter = rows // 4

    def around(value, tile, line):
        west, east = beside(value, "lon", [m[tile * rows:(tile + 1) * rows] for m in lon_in])
        south, north = beyond(value, "lat", [m[base + line:base + line + 1] for m in lat_in])
        laplace = east + west + north + south - 4.0 * value
        return value + diffusion * laplace, east - west, north - south

    new_east, _, _ = around(east[0], 0, slots)
    new_north, _, _ = around(north[0], 1, 0)
    warmed, zonal, meridional = around(warmth[0], 3, slots + 1)
    heating = jnp.concatenate(
        [heat_ends[:quarter], heat_middle[...], heat_ends[quarter:]], axis=0
    )
    east_out[0] = new_east - pressure * zonal
    north_out[0] = new_north - pressure * meridional
    temp_out[0] = warmed + heating / density[0]


def place_kernel(chunk, slots, *refs):
    got, out, sems = refs[:slots], refs[-2], refs[-1]
    rows = out.shape[2]
    quarter = rows // 4
    starts = (0, 3 * quarter) if chunk else (quarter, 2 * quarter)
    copies = [
        pltpu.make_async_copy(
            got[slot].at[:, part * quarter:(part + 1) * quarter, :],
            out.at[:, lax.axis_index("group") ^ slot, start:start + quarter, :],
            sems.at[slot, part],
        )
        for slot in range(slots)
        for part, start in enumerate(starts)
    ]
    for copy in copies:
        copy.start()
    for copy in copies:
        copy.wait()


def local(
    species_amounts,
    zonal_cell_fraction,
    meridional_cell_fraction,
    updraft_cell_fraction,
    warmth_anomaly,
    mass_per_volume,
    chemistry_iterations,
    companion_species,
    stoichiometric_rate,
    heat_yield,
):
    slots = lax.axis_size("group")
    n_lat = min(2, lax.axis_size("lat") - 1)
    n_lon = min(2, lax.axis_size("lon") - 1)
    tracers, strata, rows, width = species_amounts.shape
    half = rows // 2
    base = tracers * strata

    payload = jnp.concatenate(
        [
            zonal_cell_fraction[0],
            meridional_cell_fraction[0],
            updraft_cell_fraction[0],
            warmth_anomaly[0],
        ],
        axis=0,
    )
    payload = lax.optimization_barrier(payload)
    east, north, warmth = payload[:rows], payload[rows:2 * rows], payload[3 * rows:]
    lon_fields = neighbours([payload] * n_lon, "lon")
    payload = jnp.concatenate([payload] + [m[:rows] for m in lon_fields], axis=0)
    gathered = {hop: partner_swap(payload, hop) for hop in range(slots - 1, 0, -1)}
    winds = [payload] + [gathered[hop] for hop in range(1, slots)]

    packed = call(
        functools.partial(pack_kernel, n_lon, n_lat, 4),
        [struct(rows, width)] * n_lon
        + [struct(base, width)] * n_lat
        + [struct(tracers, strata, rows, width)],
        [HBM],
        scratch=[pltpu.SemaphoreType.DMA((4,))],
        limit=52 * 1024 * 1024,
    )(lax.optimization_barrier((species_amounts, payload))[0])
    species = packed[n_lon + n_lat]
    lon_in = neighbours(packed[:n_lon], "lon")
    lat_out = []
    for at, m in enumerate(packed[n_lon:n_lon + n_lat]):
        top = parity("lat") == at
        lines = [w[rows:2 * rows] for w in winds] + [east, warmth]
        lines = jnp.concatenate([jnp.where(top, f[rows - 1:], f[:1]) for f in lines], axis=0)
        lines = jnp.pad(lines, ((0, -lines.shape[0] % 8), (0, 0)))
        lat_out.append(jnp.concatenate([m, lines], axis=0))
    lat_out, lon_in = lax.optimization_barrier((lat_out, lon_in))
    lat_in = lat_neighbours(lat_out)

    def transport(chunk, lat_in=()):
        more = [*lat_in, heat_yield[None]] if chunk else []
        return call(
            functools.partial(transport_kernel, chunk, n_lon, n_lat, slots),
            [struct(half * tracers, width)] * slots + [struct(slots * tracers, width)] * chunk,
            [VMEM] * (1 + slots + n_lon + len(more)),
            scratch=[pltpu.VMEM((strata, rows, width), F32)],
            touched=256 * species_amounts.size if chunk else 1,
        )(species, *winds, *lon_in, *more)

    def swap_slots(blocks):
        swapped = {hop: partner_swap(blocks[hop], hop) for hop in range(slots - 1, 0, -1)}
        return [blocks[0]] + [swapped[hop] for hop in range(1, slots)]

    def chemistry(chunk, advected):
        got = call(
            functools.partial(chemistry_kernel, chunk, slots),
            [struct(tracers * half, width)] * slots + [struct(half, width)],
            [VMEM] * (slots + 5),
            scratch=[pltpu.VMEM((half, slots * tracers, width), F32)],
            flops=4 * half * width * companion_species.size,
            touched=8 * species_amounts.size,
        )(
            *[a.reshape(half, tracers, width) for a in advected],
            warmth,
            chemistry_iterations,
            companion_species,
            stoichiometric_rate,
            weight,
        )
        return got[:slots], got[slots]

    def put(chunk, blocks, partial):
        return call(
            functools.partial(place_kernel, chunk, slots),
            struct(tracers, strata, rows, width),
            [VMEM] * slots + [ANY] * len(partial),
            out_specs=ANY,
            scratch=[pltpu.SemaphoreType.DMA((slots, 2))],
            aliases={slots: 0} if partial else {},
            touched=4 * species_amounts.size,
        )(*[b.reshape(tracers, half, width) for b in blocks], *partial)

    mid = list(transport(0))
    mid[1], mid[2], lat_in = lax.optimization_barrier((mid[1], mid[2], lat_in))
    mid = swap_slots(mid)
    *end, weight = transport(1, lat_in)
    end = swap_slots(end)
    mid, heat_mid = chemistry(0, mid)
    mid = swap_slots(mid)
    end, heat_end = chemistry(1, end)
    end = swap_slots(end)
    east_out, north_out, temp_out = call(
        functools.partial(dynamics_kernel, n_lon, n_lat, base, slots),
        [struct(1, rows, width)] * 3,
        [VMEM] * (6 + n_lon + n_lat),
    )(
        zonal_cell_fraction,
        meridional_cell_fraction,
        warmth_anomaly,
        mass_per_volume,
        *lon_fields,
        *lat_in,
        heat_mid,
        heat_end,
    )
    tracers_out = put(1, end, [put(0, mid, [])])
    return (tracers_out, east_out, north_out, temp_out)


def solution(mesh):
    return jax.shard_map(
        local,
        mesh=mesh,
        in_specs=(
            P("group", None, "lat", "lon"),
            P("group", "lat", "lon"),
            P("group", "lat", "lon"),
            P("group", "lat", "lon"),
            P("group", "lat", "lon"),
            P("group", "lat", "lon"),
            P("lat", "lon"),
            P(),
            P(),
            P(),
        ),
        out_specs=(
            P("group", None, "lat", "lon"),
            P("group", "lat", "lon"),
            P("group", "lat", "lon"),
            P("group", "lat", "lon"),
        ),
        check_vma=False,
    )
```

```python
import functools

import jax
import jax.numpy as jnp
from jax import lax
from jax.experimental import pallas as pl
from jax.experimental.pallas import tpu as pltpu
from jax.sharding import PartitionSpec as P

diffusion = 0.1
pressure = 0.05
chem_step = 0.2

VMEM = pl.BlockSpec(memory_space=pltpu.VMEM)
ANY = pl.BlockSpec(memory_space=pl.ANY)
HBM = pl.BlockSpec(memory_space=pltpu.HBM)
LIMIT = 40 * 1024 * 1024
F32 = jnp.float32


def struct(*shape, dtype=F32):
    return jax.ShapeDtypeStruct(shape, dtype)


def call(kernel, out_shape, in_specs, out_specs=None, scratch=(), aliases=None, flops=1, touched=1, limit=LIMIT):
    return pl.pallas_call(
        kernel,
        out_shape=out_shape,
        in_specs=in_specs,
        out_specs=jax.tree.map(lambda _: VMEM, out_shape) if out_specs is None else out_specs,
        scratch_shapes=list(scratch),
        input_output_aliases=aliases or {},
        compiler_params=pltpu.CompilerParams(vmem_limit_bytes=limit),
        cost_estimate=pl.CostEstimate(flops=flops, bytes_accessed=touched, transcendentals=0),
    )


def parity(axis):
    return lax.rem(lax.axis_index(axis), 2)


def even_pairs(count):
    return [(i, i ^ 1) for i in range(count) if (i ^ 1) < count]


def odd_pairs(count):
    pairs = []
    for i in range(1, count - 1, 2):
        pairs += [(i, i + 1), (i + 1, i)]
    return pairs


def neighbours(messages, axis):
    count = lax.axis_size(axis)
    return [
        lax.ppermute(m, axis, pairs)
        for m, pairs in zip(messages, (even_pairs(count), odd_pairs(count)))
    ]


def lat_neighbours(messages):
    rows, columns = lax.axis_size("lat"), lax.axis_size("lon")
    if len(messages) < 2 or rows % 2 or columns % 2:
        return neighbours(messages, "lat")
    partner = dict(odd_pairs(rows))
    pairs = [
        (i * columns + j, partner[i] * columns + j if i in partner else i * columns + (j ^ 1))
        for i in range(rows)
        for j in range(columns)
    ]
    first = lax.ppermute(messages[0], "lat", even_pairs(rows))
    return [first, lax.ppermute(messages[1], ("lat", "lon"), pairs)]


def partner_swap(block, hop):
    return lax.ppermute(block, "group", [(i, i ^ hop) for i in range(lax.axis_size("group"))])


def lane_ids(shape):
    return lax.broadcasted_iota(jnp.int32, shape, len(shape) - 1)


def row_ids(shape):
    return lax.broadcasted_iota(jnp.int32, shape, len(shape) - 2)


def pack_kernel(n_lon, n_lat, parts, species_hbm, *refs):
    *outs, species, sems = refs
    tracers, strata, rows, width = species.shape
    share = tracers // parts
    copies = [
        pltpu.make_async_copy(
            species_hbm.at[pl.ds(part * share, share)],
            species.at[pl.ds(part * share, share)],
            sems.at[part],
        )
        for part in range(parts)
    ]
    for copy in copies:
        copy.start()
    lane = lane_ids((rows, width))
    flat = species.reshape(tracers * strata * rows, width)
    held = share * strata
    columns = [jnp.zeros((rows, width), F32) for _ in range(n_lon)]
    for part, copy in enumerate(copies):
        copy.wait()
        for at, message in enumerate(outs[n_lon:n_lon + n_lat]):
            edge = jnp.where(parity("lat") == at, rows - 1, 0)
            message[part * held:(part + 1) * held] = flat[
                pl.ds(part * held * rows + edge, held, stride=rows), :
            ]
        for at in range(n_lon):
            edge = jnp.where(parity("lon") == at, width - 1, 0)
            for t in range(part * share, (part + 1) * share):
                for level in range(strata):
                    place = level * tracers + t
                    turned = pltpu.roll(species[t, level], lax.rem(place - edge + width, width), 1)
                    columns[at] = jnp.where(lane == place, turned, columns[at])
    for message, block in zip(outs[:n_lon], columns):
        message[...] = block


def both_sides(axis, got):
    even = parity(axis) == 0
    if len(got) == 1:
        got = [got[0], got[0]]
    at = lax.axis_index(axis)
    low = jnp.where(even, got[1], got[0])
    high = jnp.where(even, got[0], got[1])
    return jnp.where(at > 0, low, 0.0), jnp.where(at < lax.axis_size(axis) - 1, high, 0.0)


def beside(value, axis, got):
    width = value.shape[1]
    lane = lane_ids(value.shape)
    low, high = both_sides(axis, got)
    west = pltpu.roll(jnp.where(lane == width - 1, low, value), 1, 1)
    east = pltpu.roll(jnp.where(lane == 0, high, value), width - 1, 1)
    return west, east


def beyond(value, axis, got):
    rows = value.shape[0]
    row = row_ids(value.shape)
    low, high = both_sides(axis, got)
    south = jnp.where(row == 0, low, pltpu.roll(value, 1, 0))
    north = jnp.where(row == rows - 1, high, pltpu.roll(value, rows - 1, 0))
    return south, north


def middle(value):
    quarter = value.shape[0] // 4
    return value[quarter:3 * quarter]


def ends(value):
    quarter = value.shape[0] // 4
    return jnp.concatenate([value[:quarter], value[3 * quarter:]], axis=0)


def faces(low, high):
    wind = 0.5 * (low + high)
    return jnp.maximum(wind, 0.0), jnp.minimum(wind, 0.0)


def coefficients(winds, lon_fields, upward, lat_in, base, pick):
    slots, n_lon = len(winds), len(lon_fields)
    strata, rows, width = upward.shape
    me = lax.axis_index("group")
    for slot in range(slots):
        upward[me ^ slot] = winds[slot][2 * rows:3 * rows]
    found = []
    for slot in range(slots):
        level = me ^ slot
        east = winds[slot][0:rows]
        east_last, east_next = beside(
            east, "lon", [m[slot * rows:(slot + 1) * rows] for m in lon_fields]
        )
        north = winds[slot][rows:2 * rows]
        rim = [m[base + slot:base + slot + 1] for m in lat_in] or [jnp.zeros((1, width), F32)]
        north_last, north_next = beyond(north, "lat", rim)
        up = upward[level]
        above = upward[jnp.minimum(level + 1, strata - 1)]
        below = upward[jnp.maximum(level - 1, 0)]
        has_above = jnp.where(level < strata - 1, 1.0, 0.0)
        has_below = jnp.where(level > 0, 1.0, 0.0)
        east_out, east_in = faces(east, east_next)
        west_in, west_out = faces(east_last, east)
        north_out, north_in = faces(north, north_next)
        south_in, south_out = faces(north_last, north)
        up_out, up_in = [has_above * f for f in faces(up, above)]
        down_in, down_out = [has_below * f for f in faces(below, up)]
        stay = 1.0 - (
            (east_out - west_out) + (north_out - south_out) + (up_out - down_out)
        )
        if n_lon < 2:
            lane, even = lane_ids((rows, width)), parity("lon") == 0
            east_in = jnp.where((lane == width - 1) & ~even, 0.0, east_in)
            west_in = jnp.where((lane == 0) & even, 0.0, west_in)
        found.append(
            [pick(f) for f in (stay, -east_in, west_in, -north_in, south_in, -up_in, down_in)]
        )
    return found


def combine(coefficient, here, east, west, north, south, up, down):
    stay, east_in, west_in, north_in, south_in, up_in, down_in = coefficient
    return (
        (stay * here + east_in * east)
        + (west_in * west + north_in * north)
        + (south_in * south + up_in * up)
        + down_in * down
    )


def weight_kernel(yields, weight):
    weight[...] = jnp.broadcast_to(yields[...], weight.shape[::-1]).T


def ends_kernel(n_lon, n_lat, slots, species, *refs):
    refs = list(refs)
    winds = [refs.pop(0) for _ in range(slots)]
    lon_fields = [refs.pop(0) for _ in range(n_lon)]
    lon_in = [refs.pop(0) for _ in range(n_lon)]
    lat_in = [refs.pop(0) for _ in range(n_lat)]
    outs = [refs.pop(0) for _ in range(slots)]
    upward = refs.pop(0)
    tracers, strata, rows, width = species.shape
    half = rows // 2
    quarter = rows // 4
    me = lax.axis_index("group")
    lane = lane_ids((half, width))
    row = row_ids((half, width))
    found = coefficients(winds, lon_fields, upward, lat_in, tracers * strata, ends)
    columns = [ends(m[0:rows]) for m in lon_in]
    if n_lon == 2:
        columns = both_sides("lon", columns)
    edge = jnp.where(parity("lon") == 0, width - 1, 0)

    def one(t, carry):
        for slot in range(slots):
            level = me ^ slot
            place = level * tracers + t
            if n_lon == 2:
                low = pltpu.roll(columns[0], lax.rem(width - place, width), 1)
                high = pltpu.roll(columns[1], width - 1 - place, 1)
            else:
                low = high = pltpu.roll(columns[0], lax.rem(width + edge - place, width), 1)
            above = jnp.minimum(level + 1, strata - 1)
            below = jnp.maximum(level - 1, 0)
            first, last = species[t, level, 0:half], species[t, level, half:rows]
            here = jnp.where(row < quarter, first, last)
            place = t * strata + level
            low_row, high_row = both_sides("lat", [m[pl.ds(place, 1), :] for m in lat_in])
            south = pltpu.roll(jnp.where(row < quarter - 1, first, last), 1, 0)
            south = jnp.where(row == 0, low_row, south)
            north = pltpu.roll(jnp.where(row < quarter + 1, first, last), half - 1, 0)
            north = jnp.where(row == half - 1, high_row, north)
            up = jnp.where(row < quarter, species[t, above, 0:half], species[t, above, half:rows])
            down = jnp.where(row < quarter, species[t, below, 0:half], species[t, below, half:rows])
            east = jnp.where(lane == width - 1, high, pltpu.roll(here, width - 1, 1))
            west = jnp.where(lane == 0, low, pltpu.roll(here, 1, 1))
            outs[slot][pl.ds(t, half, stride=tracers), :] = combine(
                found[slot], here, east, west, north, south, up, down
            )
        return carry

    lax.fori_loop(0, tracers, one, 0, unroll=tracers)


def strip_lanes(value, shift):
    width = value.shape[-1]
    return pltpu.roll(value, lax.rem(shift + 2 * width, width), 1)


def strip_of(turned, owner, strip, around=0):
    lane = lane_ids(turned[0].shape)
    block = lane // strip
    if around:
        block = jnp.where(lax.rem(lane, strip) == 0, block + len(turned) - 1, block + 1)
        block = lax.rem(block, len(turned))
    packed = turned[0]
    for level in range(1, len(turned)):
        packed = jnp.where(block == lax.rem(owner + level, len(turned)), turned[level], packed)
    return packed


def strip_kernel(slots, species, *outs):
    tracers, strata, rows, width = species.shape
    half, quarter = rows // 2, rows // 4
    strip = width // slots
    me = lax.axis_index("group")
    flat = species.reshape(tracers * strata * rows, width)

    def one(t, carry):
        turned = [
            strip_lanes(species[t, level, quarter:3 * quarter], strip * level)
            for level in range(strata)
        ]
        for slot in range(slots):
            outs[slot][pl.ds(pl.multiple_of(t * half, half), half), :] = strip_of(
                turned, me ^ slot, strip
            )
        return carry

    lax.fori_loop(0, tracers, one, 0, unroll=tracers)
    for at, line in enumerate((quarter - 1, 3 * quarter)):
        for group in range(tracers // half):
            turned = [
                strip_lanes(
                    flat[pl.ds((group * half * strata + level) * rows + line, half, stride=strata * rows), :],
                    strip * level,
                )
                for level in range(strata)
            ]
            base = tracers * (half + at) + group * half
            for slot in range(slots):
                outs[slot][base:base + half] = strip_of(turned, me ^ slot, strip)


def strip_rim_kernel(slots, species, *refs):
    strips, outs = refs[:slots], refs[slots:]
    tracers, strata, rows, width = species.shape
    half, quarter = rows // 2, rows // 4
    strip = width // slots
    share = strip // 2
    me = lax.axis_index("group")
    lane = lane_ids((half, width))
    done = tracers * (half + 2)
    for slot in range(slots):
        outs[slot][0:done] = strips[slot][...]
    for part in range(tracers // share):

        def one(i, rims):
            t = part * share + i
            turned = [
                strip_lanes(species[t, level, quarter:3 * quarter], strip * level)
                for level in range(strata)
            ]
            new = []
            for slot in range(slots):
                owner = me ^ slot
                rim = strip_of(turned, owner, strip, 1)
                rim = pltpu.roll(rim, 2 * i, 1)
                mine = lax.rem(lane - 2 * i + 1 + width, strip) < 2
                new.append(jnp.where(mine, rim, rims[slot]))
            return tuple(new)

        rims = lax.fori_loop(
            0, share, one, tuple(jnp.zeros((half, width), F32) for _ in range(slots)), unroll=8
        )
        for slot in range(slots):
            outs[slot][done + part * half:done + (part + 1) * half] = rims[slot]


def strip_edge_kernel(n_lon, slots, *refs):
    refs = list(refs)
    lon_in = [refs.pop(0) for _ in range(n_lon)]
    strips, outs = refs[:slots], refs[slots:]
    rows, width = lon_in[0].shape
    half = rows // 2
    strip = width // slots
    share = strip // 2
    me = lax.axis_index("group")
    lane = lane_ids((half, width))
    columns = [middle(m[...]) for m in lon_in]
    if n_lon == 2:
        sides = list(zip(both_sides("lon", columns), (False, True)))
    else:
        sides = [(columns[0], parity("lon") == 0)]
    parts = strip // share
    done = outs[0].shape[0] - parts * half
    for slot in range(slots):
        outs[slot][0:done] = strips[slot][0:done]
    for part in range(parts):
        place = slice(done + part * half, done + (part + 1) * half)
        rims = [strips[slot][place] for slot in range(slots)]
        for column, high in sides:
            beyond_edge = jnp.zeros((half, width), F32)
            for i in range(share):
                turned = strip_lanes(column, jnp.where(high, 0, -1) - (part * share + i) + 2 * i)
                mine = lax.rem(lane - 2 * i + width, strip) == jnp.where(high, 0, strip - 1)
                beyond_edge = jnp.where(mine, turned, beyond_edge)
            lanes = lax.rem(lane, 2) == jnp.where(high, 0, 1)
            for slot in range(slots):
                at_edge = (me ^ slot) == jnp.where(high, slots - 1, 0)
                rims[slot] = jnp.where(lanes & at_edge, beyond_edge, rims[slot])
        for slot in range(slots):
            outs[slot][place] = rims[slot]


def by_level(values, me, strip):
    block = lane_ids(values[0].shape) // strip
    packed = strip_lanes(values[0], strip * me)
    for slot in range(1, len(values)):
        level = me ^ slot
        turned = strip_lanes(values[slot], strip * level)
        packed = jnp.where(block == lax.rem(me + level, len(values)), turned, packed)
    return packed


def strip_react_kernel(n_lon, slots, *refs):
    refs = list(refs)
    raw = [refs.pop(0) for _ in range(slots)]
    winds = [refs.pop(0) for _ in range(slots)]
    lon_fields = [refs.pop(0) for _ in range(n_lon)]
    counts, companion, stoichiometry, weight = [refs.pop(0) for _ in range(4)]
    outs = [refs.pop(0) for _ in range(slots)]
    current, start, upward = refs
    strata, rows, width = upward.shape
    half, species = current.shape[:2]
    owned = species // slots
    strip = width // slots
    share = strip // 2
    me = lax.axis_index("group")
    lane = lane_ids((half, width))
    row = row_ids((half, width))
    found = coefficients(winds, lon_fields, upward, [], 0, middle)
    coefficient = [by_level(list(f), me, strip) for f in zip(*found)]
    first = [(me ^ slot) * owned for slot in range(slots)]
    flat = current.reshape(half * species, width)

    def one(t, carry):
        for slot in range(slots):
            block = raw[slot]
            here = block[pl.ds(pl.multiple_of(t * half, half), half), :]
            part = owned * (half + 2) + t // share * half
            rim = block[pl.ds(pl.multiple_of(part, half), half), :]
            rim = pltpu.roll(rim, lax.rem(width - 2 * lax.rem(t, share), width), 1)
            west = pltpu.roll(jnp.where(lax.rem(lane, strip) == strip - 1, rim, here), 1, 1)
            east = pltpu.roll(jnp.where(lax.rem(lane, strip) == 0, rim, here), width - 1, 1)
            south = jnp.where(row == 0, block[pl.ds(owned * half + t, 1), :], pltpu.roll(here, 1, 0))
            north = jnp.where(
                row == half - 1, block[pl.ds(owned * (half + 1) + t, 1), :], pltpu.roll(here, half - 1, 0)
            )
            up = pltpu.roll(here, width - strip, 1)
            down = pltpu.roll(here, strip, 1)
            value = combine(coefficient, here, east, west, north, south, up, down)
            flat[pl.ds(first[slot] + t, half, stride=species), :] = value
        return carry

    lax.fori_loop(0, owned, one, 0, unroll=owned)
    start[...] = current[...]
    warmth = by_level([middle(w[3 * rows:4 * rows]) for w in winds], me, strip)
    many = by_level([middle(counts[...])] * slots, me, strip)
    react(current, warmth, many, companion, stoichiometry)
    total = None
    for slot in range(slots):
        place = pl.ds(pl.multiple_of(first[slot], owned), owned)
        final = current[:, place, :]
        for r in range(half):
            outs[slot][r * owned:(r + 1) * owned] = final[r]
        part = jnp.sum(weight[place, :][None] * (final - start[:, place, :]), axis=1)
        total = part if total is None else total + part
    for slot in range(slots):
        outs[slot][owned * half:owned * half + half] = total


def strip_place_kernel(slots, *refs):
    got = refs[:slots]
    out, heat, stage, sems = refs[slots:]
    tracers, strata, rows, width = out.shape
    half, quarter = rows // 2, rows // 4
    strip = width // slots
    me = lax.axis_index("group")
    lane = lane_ids((half, width))

    def side_by_side(blocks, level):
        whole = blocks[0]
        for slot in range(1, slots):
            at = lax.rem((me ^ slot) + level, slots)
            whole = jnp.where(lane // strip == at, blocks[slot], whole)
        return strip_lanes(whole, -strip * level)

    def one(t, carry):
        blocks = [g[pl.ds(t, half, stride=tracers), :] for g in got]
        for level in range(strata):
            stage[t, level] = side_by_side(blocks, level)
        return carry

    lax.fori_loop(0, tracers, one, 0, unroll=tracers)
    copies = [
        pltpu.make_async_copy(
            stage.at[:, :, part * quarter:(part + 1) * quarter, :],
            out.at[:, :, (1 + part) * quarter:(2 + part) * quarter, :],
            sems.at[part],
        )
        for part in range(2)
    ]
    for copy in copies:
        copy.start()
    heat[...] = side_by_side([g[tracers * half:tracers * half + half] for g in got], me)
    for copy in copies:
        copy.wait()


def react(current, warmth, counts, companion, stoichiometry):
    half, species, width = current.shape
    repeats = companion.shape[0] // species
    line = lambda field: jnp.concatenate([field[r:r + 1] for r in range(half)], axis=1)
    rate = line(jax.nn.sigmoid(2.0 * warmth))
    many = line(counts)

    def substep(s, carry):
        now = jnp.concatenate([current[r] for r in range(half)], axis=1)
        pairs = jnp.dot(companion[...], now.astype(jnp.bfloat16), preferred_element_type=F32)
        quad = (pairs.reshape(repeats, species, half * width) * now[None]).astype(jnp.bfloat16)
        made = jnp.dot(
            stoichiometry[...],
            quad.reshape(repeats * species, half * width),
            preferred_element_type=F32,
        )
        after = now + chem_step * (rate * made - now)
        after = jnp.where(s < many, after, now)
        for r in range(half):
            current[r] = after[:, r * width:(r + 1) * width]
        return carry

    deepest = jnp.max(many)
    substep(0, 0)
    lax.fori_loop(1, deepest, substep, 0)


def chemistry_kernel(slots, *refs):
    refs = list(refs)
    advected = [refs.pop(0) for _ in range(slots)]
    warmth, counts, companion, stoichiometry, weight = [refs.pop(0) for _ in range(5)]
    outs = [refs.pop(0) for _ in range(slots)]
    heat, current = refs
    half, owned, width = advected[0].shape
    place = [
        pl.ds(pl.multiple_of((lax.axis_index("group") ^ slot) * owned, owned), owned)
        for slot in range(slots)
    ]
    for slot in range(slots):
        current[:, place[slot], :] = advected[slot][...]
    react(current, ends(warmth[...]), ends(counts[...]), companion, stoichiometry)
    total = None
    for slot in range(slots):
        final = current[:, place[slot], :]
        for r in range(half):
            outs[slot][pl.ds(r, owned, stride=half), :] = final[r]
        part = jnp.sum(weight[place[slot], :][None] * (final - advected[slot][...]), axis=1)
        total = part if total is None else total + part
    heat[...] = total


def dynamics_kernel(n_lon, n_lat, base, slots, east, north, warmth, density, *refs):
    refs = list(refs)
    lon_in = [refs.pop(0) for _ in range(n_lon)]
    lat_in = [refs.pop(0) for _ in range(n_lat)]
    heat_middle, heat_ends, east_out, north_out, temp_out = refs
    rows = temp_out.shape[1]
    quarter = rows // 4

    def around(value, tile, line):
        west, east = beside(value, "lon", [m[tile * rows:(tile + 1) * rows] for m in lon_in])
        south, north = beyond(value, "lat", [m[base + line:base + line + 1] for m in lat_in])
        laplace = east + west + north + south - 4.0 * value
        return value + diffusion * laplace, east - west, north - south

    new_east, _, _ = around(east[0], 0, slots)
    new_north, _, _ = around(north[0], slots, 0)
    warmed, zonal, meridional = around(warmth[0], slots + 1, slots + 1)
    heating = jnp.concatenate(
        [heat_ends[:quarter], heat_middle[...], heat_ends[quarter:]], axis=0
    )
    east_out[0] = new_east - pressure * zonal
    north_out[0] = new_north - pressure * meridional
    temp_out[0] = warmed + heating / density[0]


def place_kernel(slots, *refs):
    got, out, sems = refs[:slots], refs[-2], refs[-1]
    rows = out.shape[2]
    quarter = rows // 4
    copies = [
        pltpu.make_async_copy(
            got[slot].at[:, part * quarter:(part + 1) * quarter, :],
            out.at[:, lax.axis_index("group") ^ slot, start:start + quarter, :],
            sems.at[slot, part],
        )
        for slot in range(slots)
        for part, start in enumerate((0, 3 * quarter))
    ]
    for copy in copies:
        copy.start()
    for copy in copies:
        copy.wait()


def local(
    species_amounts,
    zonal_cell_fraction,
    meridional_cell_fraction,
    updraft_cell_fraction,
    warmth_anomaly,
    mass_per_volume,
    chemistry_iterations,
    companion_species,
    stoichiometric_rate,
    heat_yield,
):
    slots = lax.axis_size("group")
    n_lat = min(2, lax.axis_size("lat") - 1)
    n_lon = min(2, lax.axis_size("lon") - 1)
    tracers, strata, rows, width = species_amounts.shape
    half = rows // 2
    base = tracers * strata

    payload = jnp.concatenate(
        [
            zonal_cell_fraction[0],
            meridional_cell_fraction[0],
            updraft_cell_fraction[0],
            warmth_anomaly[0],
        ],
        axis=0,
    )
    payload = lax.optimization_barrier(payload)
    east, north, warmth = payload[:rows], payload[rows:2 * rows], payload[3 * rows:]
    gathered = {hop: partner_swap(payload, hop) for hop in range(slots - 1, 0, -1)}
    winds = [payload] + [gathered[hop] for hop in range(1, slots)]

    packed = call(
        functools.partial(pack_kernel, n_lon, n_lat, 4),
        [struct(rows, width)] * n_lon
        + [struct(base, width)] * n_lat
        + [struct(tracers, strata, rows, width)],
        [HBM],
        scratch=[pltpu.SemaphoreType.DMA((4,))],
        limit=52 * 1024 * 1024,
    )(species_amounts)
    species = packed[n_lon + n_lat]
    lon_in = neighbours(packed[:n_lon], "lon")
    strip = width // slots
    strips = call(
        functools.partial(strip_kernel, slots),
        [struct(tracers * (half + 2), width)] * slots,
        [VMEM],
        touched=64 * species_amounts.size,
    )(species)
    strips = call(
        functools.partial(strip_rim_kernel, slots),
        [struct(tracers * (half + 2) + tracers // (strip // 2) * half, width)] * slots,
        [VMEM] * (1 + slots),
        touched=64 * species_amounts.size,
    )(species, *strips)
    strips = call(
        functools.partial(strip_edge_kernel, n_lon, slots),
        [struct(*strips[0].shape)] * slots,
        [VMEM] * (n_lon + slots),
    )(*lon_in, *strips)
    strips, winds[1] = lax.optimization_barrier((strips, winds[1]))
    lon_fields = jnp.concatenate([w[:rows] for w in winds] + [north, warmth], axis=0)
    lon_fields = neighbours([lon_fields] * n_lon, "lon")
    lat_out = []
    for at, m in enumerate(packed[n_lon:n_lon + n_lat]):
        top = parity("lat") == at
        lines = [w[rows:2 * rows] for w in winds] + [east, warmth]
        lines = jnp.concatenate([jnp.where(top, f[rows - 1:], f[:1]) for f in lines], axis=0)
        lines = jnp.pad(lines, ((0, -lines.shape[0] % 8), (0, 0)))
        lat_out.append(jnp.concatenate([m, lines], axis=0))
    lat_out, lon_fields = lax.optimization_barrier((lat_out, lon_fields))
    lat_in = lat_neighbours(lat_out)

    def swap_slots(blocks):
        swapped = {hop: partner_swap(blocks[hop], hop) for hop in range(slots - 1, 0, -1)}
        return [blocks[0]] + [swapped[hop] for hop in range(1, slots)]

    strips = swap_slots(strips)
    weight = call(
        weight_kernel, struct(slots * tracers, width), [VMEM], touched=256 * species_amounts.size
    )(heat_yield[None])
    weight, lat_in = lax.optimization_barrier((weight, lat_in))
    adv = call(
        functools.partial(ends_kernel, n_lon, n_lat, slots),
        [struct(half * tracers, width)] * slots,
        [VMEM] * (1 + slots + 2 * n_lon + n_lat),
        scratch=[pltpu.VMEM((strata, rows, width), F32)],
        touched=256 * species_amounts.size,
    )(species, *winds, *lon_fields, *lon_in, *lat_in)
    adv = swap_slots(adv)
    reacted = call(
        functools.partial(strip_react_kernel, n_lon, slots),
        [struct(tracers * half + half, width)] * slots,
        [VMEM] * (2 * slots + n_lon + 4),
        scratch=[
            pltpu.VMEM((half, slots * tracers, width), F32),
            pltpu.VMEM((half, slots * tracers, width), F32),
            pltpu.VMEM((strata, rows, width), F32),
        ],
        flops=4 * half * width * companion_species.size,
        touched=8 * species_amounts.size,
    )(*strips, *winds, *lon_fields, chemistry_iterations, companion_species, stoichiometric_rate, weight)
    reacted = swap_slots(reacted)
    *end, heat_end = call(
        functools.partial(chemistry_kernel, slots),
        [struct(tracers * half, width)] * slots + [struct(half, width)],
        [VMEM] * (slots + 5),
        scratch=[pltpu.VMEM((half, slots * tracers, width), F32)],
        flops=4 * half * width * companion_species.size,
        touched=8 * species_amounts.size,
    )(
        *[a.reshape(half, tracers, width) for a in adv],
        warmth,
        chemistry_iterations,
        companion_species,
        stoichiometric_rate,
        weight,
    )
    end = swap_slots(end)
    partial, heat_mid = call(
        functools.partial(strip_place_kernel, slots),
        [struct(tracers, strata, rows, width), struct(half, width)],
        [VMEM] * slots,
        out_specs=[ANY, VMEM],
        scratch=[pltpu.VMEM((tracers, strata, half, width), F32), pltpu.SemaphoreType.DMA((2,))],
        touched=4 * species_amounts.size,
    )(*reacted)
    east_out, north_out, temp_out = call(
        functools.partial(dynamics_kernel, n_lon, n_lat, base, slots),
        [struct(1, rows, width)] * 3,
        [VMEM] * (6 + n_lon + n_lat),
    )(
        zonal_cell_fraction,
        meridional_cell_fraction,
        warmth_anomaly,
        mass_per_volume,
        *lon_fields,
        *lat_in,
        heat_mid,
        heat_end,
    )
    tracers_out = call(
        functools.partial(place_kernel, slots),
        struct(tracers, strata, rows, width),
        [VMEM] * slots + [ANY],
        out_specs=ANY,
        scratch=[pltpu.SemaphoreType.DMA((slots, 2))],
        aliases={slots: 0},
        touched=4 * species_amounts.size,
    )(*[b.reshape(tracers, half, width) for b in end], partial)
    return (tracers_out, east_out, north_out, temp_out)


def solution(mesh):
    return jax.shard_map(
        local,
        mesh=mesh,
        in_specs=(
            P("group", None, "lat", "lon"),
            P("group", "lat", "lon"),
            P("group", "lat", "lon"),
            P("group", "lat", "lon"),
            P("group", "lat", "lon"),
            P("group", "lat", "lon"),
            P("lat", "lon"),
            P(),
            P(),
            P(),
        ),
        out_specs=(
            P("group", None, "lat", "lon"),
            P("group", "lat", "lon"),
            P("group", "lat", "lon"),
            P("group", "lat", "lon"),
        ),
        check_vma=False,
    )
```

```python
import functools

import jax
import jax.numpy as jnp
from jax import lax
from jax.experimental import pallas as pl
from jax.experimental.pallas import tpu as pltpu
from jax.sharding import PartitionSpec as P

diffusion = 0.1
pressure = 0.05
chem_step = 0.2

VMEM = pl.BlockSpec(memory_space=pltpu.VMEM)
ANY = pl.BlockSpec(memory_space=pl.ANY)
HBM = pl.BlockSpec(memory_space=pltpu.HBM)
LIMIT = 40 * 1024 * 1024
F32 = jnp.float32


def struct(*shape, dtype=F32):
    return jax.ShapeDtypeStruct(shape, dtype)


def call(kernel, out_shape, in_specs, out_specs=None, scratch=(), aliases=None, flops=1, touched=1, limit=LIMIT):
    return pl.pallas_call(
        kernel,
        out_shape=out_shape,
        in_specs=in_specs,
        out_specs=jax.tree.map(lambda _: VMEM, out_shape) if out_specs is None else out_specs,
        scratch_shapes=list(scratch),
        input_output_aliases=aliases or {},
        compiler_params=pltpu.CompilerParams(vmem_limit_bytes=limit),
        cost_estimate=pl.CostEstimate(flops=flops, bytes_accessed=touched, transcendentals=0),
    )


def parity(axis):
    return lax.rem(lax.axis_index(axis), 2)


def even_pairs(count):
    return [(i, i ^ 1) for i in range(count) if (i ^ 1) < count]


def odd_pairs(count):
    pairs = []
    for i in range(1, count - 1, 2):
        pairs += [(i, i + 1), (i + 1, i)]
    return pairs


def neighbours(messages, axis):
    count = lax.axis_size(axis)
    return [
        lax.ppermute(m, axis, pairs)
        for m, pairs in zip(messages, (even_pairs(count), odd_pairs(count)))
    ]


def lat_neighbours(messages):
    rows, columns = lax.axis_size("lat"), lax.axis_size("lon")
    if len(messages) < 2 or rows % 2 or columns % 2:
        return neighbours(messages, "lat")
    partner = dict(odd_pairs(rows))
    pairs = [
        (i * columns + j, partner[i] * columns + j if i in partner else i * columns + (j ^ 1))
        for i in range(rows)
        for j in range(columns)
    ]
    first = lax.ppermute(messages[0], "lat", even_pairs(rows))
    return [first, lax.ppermute(messages[1], ("lat", "lon"), pairs)]


def partner_swap(block, hop):
    return lax.ppermute(block, "group", [(i, i ^ hop) for i in range(lax.axis_size("group"))])


def lane_ids(shape):
    return lax.broadcasted_iota(jnp.int32, shape, len(shape) - 1)


def row_ids(shape):
    return lax.broadcasted_iota(jnp.int32, shape, len(shape) - 2)


def pack_kernel(n_lon, n_lat, parts, species_hbm, *refs):
    *outs, species, sems = refs
    tracers, strata, rows, width = species.shape
    share = tracers // parts
    copies = [
        pltpu.make_async_copy(
            species_hbm.at[pl.ds(part * share, share)],
            species.at[pl.ds(part * share, share)],
            sems.at[part],
        )
        for part in range(parts)
    ]
    for copy in copies:
        copy.start()
    lane = lane_ids((rows, width))
    flat = species.reshape(tracers * strata * rows, width)
    held = share * strata
    columns = [jnp.zeros((rows, width), F32) for _ in range(n_lon)]
    for part, copy in enumerate(copies):
        copy.wait()
        for at, message in enumerate(outs[n_lon:n_lon + n_lat]):
            edge = jnp.where(parity("lat") == at, rows - 1, 0)
            message[part * held:(part + 1) * held] = flat[
                pl.ds(part * held * rows + edge, held, stride=rows), :
            ]
        for at in range(n_lon):
            edge = jnp.where(parity("lon") == at, width - 1, 0)
            for t in range(part * share, (part + 1) * share):
                for level in range(strata):
                    place = level * tracers + t
                    turned = pltpu.roll(species[t, level], lax.rem(place - edge + width, width), 1)
                    columns[at] = jnp.where(lane == place, turned, columns[at])
    for message, block in zip(outs[:n_lon], columns):
        message[...] = block


def both_sides(axis, got):
    even = parity(axis) == 0
    if len(got) == 1:
        got = [got[0], got[0]]
    at = lax.axis_index(axis)
    low = jnp.where(even, got[1], got[0])
    high = jnp.where(even, got[0], got[1])
    return jnp.where(at > 0, low, 0.0), jnp.where(at < lax.axis_size(axis) - 1, high, 0.0)


def beside(value, axis, got):
    width = value.shape[1]
    lane = lane_ids(value.shape)
    low, high = both_sides(axis, got)
    west = pltpu.roll(jnp.where(lane == width - 1, low, value), 1, 1)
    east = pltpu.roll(jnp.where(lane == 0, high, value), width - 1, 1)
    return west, east


def beyond(value, axis, got):
    rows = value.shape[0]
    row = row_ids(value.shape)
    low, high = both_sides(axis, got)
    south = jnp.where(row == 0, low, pltpu.roll(value, 1, 0))
    north = jnp.where(row == rows - 1, high, pltpu.roll(value, rows - 1, 0))
    return south, north


def middle(value):
    quarter = value.shape[0] // 4
    return value[quarter:3 * quarter]


def ends(value):
    quarter = value.shape[0] // 4
    return jnp.concatenate([value[:quarter], value[3 * quarter:]], axis=0)


def faces(low, high):
    wind = 0.5 * (low + high)
    return jnp.maximum(wind, 0.0), jnp.minimum(wind, 0.0)


def coefficients(winds, lon_fields, upward, lat_in, base, pick):
    slots, n_lon = len(winds), len(lon_fields)
    strata, rows, width = upward.shape
    me = lax.axis_index("group")
    for slot in range(slots):
        upward[me ^ slot] = winds[slot][2 * rows:3 * rows]
    found = []
    for slot in range(slots):
        level = me ^ slot
        east = winds[slot][0:rows]
        east_last, east_next = beside(
            east, "lon", [m[slot * rows:(slot + 1) * rows] for m in lon_fields]
        )
        north = winds[slot][rows:2 * rows]
        rim = [m[base + slot:base + slot + 1] for m in lat_in] or [jnp.zeros((1, width), F32)]
        north_last, north_next = beyond(north, "lat", rim)
        up = upward[level]
        above = upward[jnp.minimum(level + 1, strata - 1)]
        below = upward[jnp.maximum(level - 1, 0)]
        has_above = jnp.where(level < strata - 1, 1.0, 0.0)
        has_below = jnp.where(level > 0, 1.0, 0.0)
        east_out, east_in = faces(east, east_next)
        west_in, west_out = faces(east_last, east)
        north_out, north_in = faces(north, north_next)
        south_in, south_out = faces(north_last, north)
        up_out, up_in = [has_above * f for f in faces(up, above)]
        down_in, down_out = [has_below * f for f in faces(below, up)]
        stay = 1.0 - (
            (east_out - west_out) + (north_out - south_out) + (up_out - down_out)
        )
        if n_lon < 2:
            lane, even = lane_ids((rows, width)), parity("lon") == 0
            east_in = jnp.where((lane == width - 1) & ~even, 0.0, east_in)
            west_in = jnp.where((lane == 0) & even, 0.0, west_in)
        found.append(
            [pick(f) for f in (stay, -east_in, west_in, -north_in, south_in, -up_in, down_in)]
        )
    return found


def combine(coefficient, here, east, west, north, south, up, down):
    stay, east_in, west_in, north_in, south_in, up_in, down_in = coefficient
    return (
        (stay * here + east_in * east)
        + (west_in * west + north_in * north)
        + (south_in * south + up_in * up)
        + down_in * down
    )


def weight_kernel(yields, weight):
    weight[...] = jnp.broadcast_to(yields[...], weight.shape[::-1]).T


def ends_kernel(n_lon, slots, species, *refs):
    refs = list(refs)
    winds = [refs.pop(0) for _ in range(slots)]
    lon_fields = [refs.pop(0) for _ in range(n_lon)]
    lon_in = [refs.pop(0) for _ in range(n_lon)]
    outs = [refs.pop(0) for _ in range(slots)]
    upward = refs.pop(0)
    tracers, strata, rows, width = species.shape
    half = rows // 2
    quarter = rows // 4
    me = lax.axis_index("group")
    lane = lane_ids((half, width))
    row = row_ids((half, width))
    found = coefficients(winds, lon_fields, upward, [], 0, ends)
    columns = [ends(m[0:rows]) for m in lon_in]
    if n_lon == 2:
        columns = both_sides("lon", columns)
    edge = jnp.where(parity("lon") == 0, width - 1, 0)

    def one(t, carry):
        for slot in range(slots):
            level = me ^ slot
            place = level * tracers + t
            if n_lon == 2:
                low = pltpu.roll(columns[0], lax.rem(width - place, width), 1)
                high = pltpu.roll(columns[1], width - 1 - place, 1)
            else:
                low = high = pltpu.roll(columns[0], lax.rem(width + edge - place, width), 1)
            above = jnp.minimum(level + 1, strata - 1)
            below = jnp.maximum(level - 1, 0)
            first, last = species[t, level, 0:half], species[t, level, half:rows]
            here = jnp.where(row < quarter, first, last)
            south = pltpu.roll(jnp.where(row < quarter - 1, first, last), 1, 0)
            south = jnp.where(row == 0, 0.0, south)
            north = pltpu.roll(jnp.where(row < quarter + 1, first, last), half - 1, 0)
            north = jnp.where(row == half - 1, 0.0, north)
            up = jnp.where(row < quarter, species[t, above, 0:half], species[t, above, half:rows])
            down = jnp.where(row < quarter, species[t, below, 0:half], species[t, below, half:rows])
            east = jnp.where(lane == width - 1, high, pltpu.roll(here, width - 1, 1))
            west = jnp.where(lane == 0, low, pltpu.roll(here, 1, 1))
            outs[slot][pl.ds(t, half, stride=tracers), :] = combine(
                found[slot], here, east, west, north, south, up, down
            )
        return carry

    lax.fori_loop(0, tracers, one, 0, unroll=tracers)


def ends_rim_kernel(n_lat, slots, species, *refs):
    refs = list(refs)
    winds = [refs.pop(0) for _ in range(slots)]
    lat_in = [refs.pop(0) for _ in range(n_lat)]
    before, outs = refs[:slots], refs[slots:]
    tracers, strata, rows, width = species.shape
    held = before[0].shape[0]
    base = tracers * strata
    me = lax.axis_index("group")
    flat = species.reshape(base * rows, width)
    for slot in range(slots):
        level = me ^ slot
        here = [
            flat[pl.ds(level * rows + line, tracers, stride=strata * rows), :]
            for line in (0, rows - 1)
        ]
        low, high = both_sides(
            "lat", [m[pl.ds(level, tracers, stride=strata), :] for m in lat_in]
        )
        low_wind, high_wind = both_sides("lat", [m[base + slot:base + slot + 1] for m in lat_in])
        first, last = winds[slot][rows:rows + 1], winds[slot][2 * rows - 1:2 * rows]
        came, went = faces(low_wind, first)
        south = (went - jnp.minimum(0.5 * first, 0.0)) * here[0] + came * low
        went, came = faces(last, high_wind)
        north = (went - jnp.maximum(0.5 * last, 0.0)) * here[1] + came * high
        outs[slot][0:tracers] = before[slot][0:tracers] + south
        outs[slot][tracers:held - tracers] = before[slot][tracers:held - tracers]
        outs[slot][held - tracers:held] = before[slot][held - tracers:held] - north


def strip_lanes(value, shift):
    width = value.shape[-1]
    return pltpu.roll(value, lax.rem(shift + 2 * width, width), 1)


def strip_of(turned, owner, strip, around=0):
    lane = lane_ids(turned[0].shape)
    block = lane // strip
    if around:
        block = jnp.where(lax.rem(lane, strip) == 0, block + len(turned) - 1, block + 1)
        block = lax.rem(block, len(turned))
    packed = turned[0]
    for level in range(1, len(turned)):
        packed = jnp.where(block == lax.rem(owner + level, len(turned)), turned[level], packed)
    return packed


def strip_kernel(slots, species, *outs):
    tracers, strata, rows, width = species.shape
    half, quarter = rows // 2, rows // 4
    strip = width // slots
    me = lax.axis_index("group")
    flat = species.reshape(tracers * strata * rows, width)

    def one(t, carry):
        turned = [
            strip_lanes(species[t, level, quarter:3 * quarter], strip * level)
            for level in range(strata)
        ]
        for slot in range(slots):
            outs[slot][pl.ds(pl.multiple_of(t * half, half), half), :] = strip_of(
                turned, me ^ slot, strip
            )
        return carry

    lax.fori_loop(0, tracers, one, 0, unroll=tracers)
    for at, line in enumerate((quarter - 1, 3 * quarter)):
        for group in range(tracers // half):
            turned = [
                strip_lanes(
                    flat[pl.ds((group * half * strata + level) * rows + line, half, stride=strata * rows), :],
                    strip * level,
                )
                for level in range(strata)
            ]
            base = tracers * (half + at) + group * half
            for slot in range(slots):
                outs[slot][base:base + half] = strip_of(turned, me ^ slot, strip)


def strip_rim_kernel(slots, species, *refs):
    strips, outs = refs[:slots], refs[slots:]
    tracers, strata, rows, width = species.shape
    half, quarter = rows // 2, rows // 4
    strip = width // slots
    share = strip // 2
    me = lax.axis_index("group")
    lane = lane_ids((half, width))
    done = tracers * (half + 2)
    for slot in range(slots):
        outs[slot][0:done] = strips[slot][...]
    parts = tracers // share

    def one(i, rims):
        new = []
        for part in range(parts):
            turned = [
                strip_lanes(species[part * share + i, level, quarter:3 * quarter], strip * level)
                for level in range(strata)
            ]
            for slot in range(slots):
                rim = pltpu.roll(strip_of(turned, me ^ slot, strip, 1), 2 * i, 1)
                mine = lax.rem(lane - 2 * i + 1 + width, strip) < 2
                new.append(jnp.where(mine, rim, rims[part * slots + slot]))
        return tuple(new)

    rims = lax.fori_loop(
        0,
        share,
        one,
        tuple(jnp.zeros((half, width), F32) for _ in range(parts * slots)),
        unroll=8,
    )
    for part in range(parts):
        for slot in range(slots):
            outs[slot][done + part * half:done + (part + 1) * half] = rims[part * slots + slot]


def strip_edge_kernel(n_lon, slots, *refs):
    refs = list(refs)
    lon_in = [refs.pop(0) for _ in range(n_lon)]
    strips, outs = refs[:slots], refs[slots:]
    rows, width = lon_in[0].shape
    half = rows // 2
    strip = width // slots
    share = strip // 2
    me = lax.axis_index("group")
    lane = lane_ids((half, width))
    columns = [middle(m[...]) for m in lon_in]
    if n_lon == 2:
        sides = list(zip(both_sides("lon", columns), (False, True)))
    else:
        sides = [(columns[0], parity("lon") == 0)]
    parts = strip // share
    done = outs[0].shape[0] - parts * half
    for slot in range(slots):
        outs[slot][0:done] = strips[slot][0:done]
    for part in range(parts):
        place = slice(done + part * half, done + (part + 1) * half)
        rims = [strips[slot][place] for slot in range(slots)]
        for column, high in sides:
            beyond_edge = jnp.zeros((half, width), F32)
            for i in range(share):
                turned = strip_lanes(column, jnp.where(high, 0, -1) - (part * share + i) + 2 * i)
                mine = lax.rem(lane - 2 * i + width, strip) == jnp.where(high, 0, strip - 1)
                beyond_edge = jnp.where(mine, turned, beyond_edge)
            lanes = lax.rem(lane, 2) == jnp.where(high, 0, 1)
            for slot in range(slots):
                at_edge = (me ^ slot) == jnp.where(high, slots - 1, 0)
                rims[slot] = jnp.where(lanes & at_edge, beyond_edge, rims[slot])
        for slot in range(slots):
            outs[slot][place] = rims[slot]


def by_level(values, me, strip):
    block = lane_ids(values[0].shape) // strip
    packed = strip_lanes(values[0], strip * me)
    for slot in range(1, len(values)):
        level = me ^ slot
        turned = strip_lanes(values[slot], strip * level)
        packed = jnp.where(block == lax.rem(me + level, len(values)), turned, packed)
    return packed


def strip_react_kernel(n_lon, slots, *refs):
    refs = list(refs)
    raw = [refs.pop(0) for _ in range(slots)]
    winds = [refs.pop(0) for _ in range(slots)]
    lon_fields = [refs.pop(0) for _ in range(n_lon)]
    counts, companion, stoichiometry, weight = [refs.pop(0) for _ in range(4)]
    outs = [refs.pop(0) for _ in range(slots)]
    current, start, upward = refs
    strata, rows, width = upward.shape
    half, species = current.shape[:2]
    owned = species // slots
    strip = width // slots
    share = strip // 2
    me = lax.axis_index("group")
    lane = lane_ids((half, width))
    row = row_ids((half, width))
    found = coefficients(winds, lon_fields, upward, [], 0, middle)
    coefficient = [by_level(list(f), me, strip) for f in zip(*found)]
    first = [(me ^ slot) * owned for slot in range(slots)]
    flat = current.reshape(half * species, width)

    def one(t, carry):
        for slot in range(slots):
            block = raw[slot]
            here = block[pl.ds(pl.multiple_of(t * half, half), half), :]
            part = owned * (half + 2) + t // share * half
            rim = block[pl.ds(pl.multiple_of(part, half), half), :]
            rim = pltpu.roll(rim, lax.rem(width - 2 * lax.rem(t, share), width), 1)
            west = pltpu.roll(jnp.where(lax.rem(lane, strip) == strip - 1, rim, here), 1, 1)
            east = pltpu.roll(jnp.where(lax.rem(lane, strip) == 0, rim, here), width - 1, 1)
            south = jnp.where(row == 0, block[pl.ds(owned * half + t, 1), :], pltpu.roll(here, 1, 0))
            north = jnp.where(
                row == half - 1, block[pl.ds(owned * (half + 1) + t, 1), :], pltpu.roll(here, half - 1, 0)
            )
            up = pltpu.roll(here, width - strip, 1)
            down = pltpu.roll(here, strip, 1)
            value = combine(coefficient, here, east, west, north, south, up, down)
            flat[pl.ds(first[slot] + t, half, stride=species), :] = value
        return carry

    lax.fori_loop(0, owned, one, 0, unroll=owned)
    start[...] = current[...]
    warmth = by_level([middle(w[3 * rows:4 * rows]) for w in winds], me, strip)
    many = by_level([middle(counts[...])] * slots, me, strip)
    react(current, warmth, many, companion, stoichiometry)
    total = None
    for slot in range(slots):
        place = pl.ds(pl.multiple_of(first[slot], owned), owned)
        final = current[:, place, :]
        for r in range(half):
            outs[slot][r * owned:(r + 1) * owned] = final[r]
        part = jnp.sum(weight[place, :][None] * (final - start[:, place, :]), axis=1)
        total = part if total is None else total + part
    for slot in range(slots):
        outs[slot][owned * half:owned * half + half] = total


def strip_place_kernel(slots, *refs):
    got = refs[:slots]
    out, heat, stage, sems = refs[slots:]
    tracers, strata, rows, width = out.shape
    half, quarter = rows // 2, rows // 4
    strip = width // slots
    me = lax.axis_index("group")
    lane = lane_ids((half, width))

    def side_by_side(blocks, level):
        whole = blocks[0]
        for slot in range(1, slots):
            at = lax.rem((me ^ slot) + level, slots)
            whole = jnp.where(lane // strip == at, blocks[slot], whole)
        return strip_lanes(whole, -strip * level)

    def one(t, carry):
        blocks = [g[pl.ds(t, half, stride=tracers), :] for g in got]
        for level in range(strata):
            stage[t, level] = side_by_side(blocks, level)
        return carry

    lax.fori_loop(0, tracers, one, 0, unroll=tracers)
    copies = [
        pltpu.make_async_copy(
            stage.at[:, :, part * quarter:(part + 1) * quarter, :],
            out.at[:, :, (1 + part) * quarter:(2 + part) * quarter, :],
            sems.at[part],
        )
        for part in range(2)
    ]
    for copy in copies:
        copy.start()
    heat[...] = side_by_side([g[tracers * half:tracers * half + half] for g in got], me)
    for copy in copies:
        copy.wait()


def react(current, warmth, counts, companion, stoichiometry):
    half, species, width = current.shape
    repeats = companion.shape[0] // species
    line = lambda field: jnp.concatenate([field[r:r + 1] for r in range(half)], axis=1)
    rate = line(jax.nn.sigmoid(2.0 * warmth))
    many = line(counts)

    def substep(s, carry):
        now = jnp.concatenate([current[r] for r in range(half)], axis=1)
        pairs = jnp.dot(companion[...], now.astype(jnp.bfloat16), preferred_element_type=F32)
        quad = (pairs.reshape(repeats, species, half * width) * now[None]).astype(jnp.bfloat16)
        made = jnp.dot(
            stoichiometry[...],
            quad.reshape(repeats * species, half * width),
            preferred_element_type=F32,
        )
        after = now + chem_step * (rate * made - now)
        after = jnp.where(s < many, after, now)
        for r in range(half):
            current[r] = after[:, r * width:(r + 1) * width]
        return carry

    deepest = jnp.max(many)
    substep(0, 0)
    lax.fori_loop(1, deepest, substep, 0)


def chemistry_kernel(slots, *refs):
    refs = list(refs)
    advected = [refs.pop(0) for _ in range(slots)]
    warmth, counts, companion, stoichiometry, weight = [refs.pop(0) for _ in range(5)]
    outs = [refs.pop(0) for _ in range(slots)]
    heat, current = refs
    half, owned, width = advected[0].shape
    place = [
        pl.ds(pl.multiple_of((lax.axis_index("group") ^ slot) * owned, owned), owned)
        for slot in range(slots)
    ]
    for slot in range(slots):
        current[:, place[slot], :] = advected[slot][...]
    react(current, ends(warmth[...]), ends(counts[...]), companion, stoichiometry)
    total = None
    for slot in range(slots):
        final = current[:, place[slot], :]
        for r in range(half):
            outs[slot][pl.ds(r, owned, stride=half), :] = final[r]
        part = jnp.sum(weight[place[slot], :][None] * (final - advected[slot][...]), axis=1)
        total = part if total is None else total + part
    heat[...] = total


def dynamics_kernel(n_lon, n_lat, base, slots, east, north, warmth, density, *refs):
    refs = list(refs)
    lon_in = [refs.pop(0) for _ in range(n_lon)]
    lat_in = [refs.pop(0) for _ in range(n_lat)]
    heat_middle, heat_ends, east_out, north_out, temp_out = refs
    rows = temp_out.shape[1]
    quarter = rows // 4

    def around(value, tile, line):
        west, east = beside(value, "lon", [m[tile * rows:(tile + 1) * rows] for m in lon_in])
        south, north = beyond(value, "lat", [m[base + line:base + line + 1] for m in lat_in])
        laplace = east + west + north + south - 4.0 * value
        return value + diffusion * laplace, east - west, north - south

    new_east, _, _ = around(east[0], 0, slots)
    new_north, _, _ = around(north[0], slots, 0)
    warmed, zonal, meridional = around(warmth[0], slots + 1, slots + 1)
    heating = jnp.concatenate(
        [heat_ends[:quarter], heat_middle[...], heat_ends[quarter:]], axis=0
    )
    east_out[0] = new_east - pressure * zonal
    north_out[0] = new_north - pressure * meridional
    temp_out[0] = warmed + heating / density[0]


def place_kernel(slots, *refs):
    got, out, sems = refs[:slots], refs[-2], refs[-1]
    rows = out.shape[2]
    quarter = rows // 4
    copies = [
        pltpu.make_async_copy(
            got[slot].at[:, part * quarter:(part + 1) * quarter, :],
            out.at[:, lax.axis_index("group") ^ slot, start:start + quarter, :],
            sems.at[slot, part],
        )
        for slot in range(slots)
        for part, start in enumerate((0, 3 * quarter))
    ]
    for copy in copies:
        copy.start()
    for copy in copies:
        copy.wait()


def local(
    species_amounts,
    zonal_cell_fraction,
    meridional_cell_fraction,
    updraft_cell_fraction,
    warmth_anomaly,
    mass_per_volume,
    chemistry_iterations,
    companion_species,
    stoichiometric_rate,
    heat_yield,
):
    slots = lax.axis_size("group")
    n_lat = min(2, lax.axis_size("lat") - 1)
    n_lon = min(2, lax.axis_size("lon") - 1)
    tracers, strata, rows, width = species_amounts.shape
    half = rows // 2
    base = tracers * strata

    payload = jnp.concatenate(
        [
            zonal_cell_fraction[0],
            meridional_cell_fraction[0],
            updraft_cell_fraction[0],
            warmth_anomaly[0],
        ],
        axis=0,
    )
    payload = lax.optimization_barrier(payload)
    east, north, warmth = payload[:rows], payload[rows:2 * rows], payload[3 * rows:]
    gathered = {hop: partner_swap(payload, hop) for hop in range(slots - 1, 0, -1)}
    winds = [payload] + [gathered[hop] for hop in range(1, slots)]

    packed = call(
        functools.partial(pack_kernel, n_lon, n_lat, 4),
        [struct(rows, width)] * n_lon
        + [struct(base, width)] * n_lat
        + [struct(tracers, strata, rows, width)],
        [HBM],
        scratch=[pltpu.SemaphoreType.DMA((4,))],
        limit=52 * 1024 * 1024,
    )(species_amounts)
    species = packed[n_lon + n_lat]
    lon_in = neighbours(packed[:n_lon], "lon")
    strip = width // slots
    strips = call(
        functools.partial(strip_kernel, slots),
        [struct(tracers * (half + 2), width)] * slots,
        [VMEM],
        touched=64 * species_amounts.size,
    )(species)
    strips = call(
        functools.partial(strip_rim_kernel, slots),
        [struct(tracers * (half + 2) + tracers // (strip // 2) * half, width)] * slots,
        [VMEM] * (1 + slots),
        touched=64 * species_amounts.size,
    )(species, *strips)
    strips = call(
        functools.partial(strip_edge_kernel, n_lon, slots),
        [struct(*strips[0].shape)] * slots,
        [VMEM] * (n_lon + slots),
    )(*lon_in, *strips)
    strips, winds[1] = lax.optimization_barrier((strips, winds[1]))
    lon_fields = jnp.concatenate([w[:rows] for w in winds] + [north, warmth], axis=0)
    lon_fields = neighbours([lon_fields] * n_lon, "lon")
    lat_out = []
    for at, m in enumerate(packed[n_lon:n_lon + n_lat]):
        top = parity("lat") == at
        lines = [w[rows:2 * rows] for w in winds] + [east, warmth]
        lines = jnp.concatenate([jnp.where(top, f[rows - 1:], f[:1]) for f in lines], axis=0)
        lines = jnp.pad(lines, ((0, -lines.shape[0] % 8), (0, 0)))
        lat_out.append(jnp.concatenate([m, lines], axis=0))
    lat_out, lon_fields = lax.optimization_barrier((lat_out, lon_fields))
    lat_in = lat_neighbours(lat_out)

    def swap_slots(blocks):
        swapped = {hop: partner_swap(blocks[hop], hop) for hop in range(slots - 1, 0, -1)}
        return [blocks[0]] + [swapped[hop] for hop in range(1, slots)]

    strips = swap_slots(strips)
    weight = call(
        weight_kernel, struct(slots * tracers, width), [VMEM], touched=256 * species_amounts.size
    )(heat_yield[None])
    adv = call(
        functools.partial(ends_kernel, n_lon, slots),
        [struct(half * tracers, width)] * slots,
        [VMEM] * (1 + slots + 2 * n_lon),
        scratch=[pltpu.VMEM((strata, rows, width), F32)],
        touched=256 * species_amounts.size,
    )(species, *winds, *lon_fields, *lon_in)
    weight, lat_in = lax.optimization_barrier((weight, lat_in))
    adv = call(
        functools.partial(ends_rim_kernel, n_lat, slots),
        [struct(half * tracers, width)] * slots,
        [VMEM] * (1 + 2 * slots + n_lat),
    )(species, *winds, *lat_in, *adv)
    adv = swap_slots(adv)
    reacted = call(
        functools.partial(strip_react_kernel, n_lon, slots),
        [struct(tracers * half + half, width)] * slots,
        [VMEM] * (2 * slots + n_lon + 4),
        scratch=[
            pltpu.VMEM((half, slots * tracers, width), F32),
            pltpu.VMEM((half, slots * tracers, width), F32),
            pltpu.VMEM((strata, rows, width), F32),
        ],
        flops=4 * half * width * companion_species.size,
        touched=8 * species_amounts.size,
    )(*strips, *winds, *lon_fields, chemistry_iterations, companion_species, stoichiometric_rate, weight)
    reacted = swap_slots(reacted)
    *end, heat_end = call(
        functools.partial(chemistry_kernel, slots),
        [struct(tracers * half, width)] * slots + [struct(half, width)],
        [VMEM] * (slots + 5),
        scratch=[pltpu.VMEM((half, slots * tracers, width), F32)],
        flops=4 * half * width * companion_species.size,
        touched=8 * species_amounts.size,
    )(
        *[a.reshape(half, tracers, width) for a in adv],
        warmth,
        chemistry_iterations,
        companion_species,
        stoichiometric_rate,
        weight,
    )
    end = swap_slots(end)
    partial, heat_mid = call(
        functools.partial(strip_place_kernel, slots),
        [struct(tracers, strata, rows, width), struct(half, width)],
        [VMEM] * slots,
        out_specs=[ANY, VMEM],
        scratch=[pltpu.VMEM((tracers, strata, half, width), F32), pltpu.SemaphoreType.DMA((2,))],
        touched=4 * species_amounts.size,
    )(*reacted)
    east_out, north_out, temp_out = call(
        functools.partial(dynamics_kernel, n_lon, n_lat, base, slots),
        [struct(1, rows, width)] * 3,
        [VMEM] * (6 + n_lon + n_lat),
    )(
        zonal_cell_fraction,
        meridional_cell_fraction,
        warmth_anomaly,
        mass_per_volume,
        *lon_fields,
        *lat_in,
        heat_mid,
        heat_end,
    )
    tracers_out = call(
        functools.partial(place_kernel, slots),
        struct(tracers, strata, rows, width),
        [VMEM] * slots + [ANY],
        out_specs=ANY,
        scratch=[pltpu.SemaphoreType.DMA((slots, 2))],
        aliases={slots: 0},
        touched=4 * species_amounts.size,
    )(*[b.reshape(tracers, half, width) for b in end], partial)
    return (tracers_out, east_out, north_out, temp_out)


def solution(mesh):
    return jax.shard_map(
        local,
        mesh=mesh,
        in_specs=(
            P("group", None, "lat", "lon"),
            P("group", "lat", "lon"),
            P("group", "lat", "lon"),
            P("group", "lat", "lon"),
            P("group", "lat", "lon"),
            P("group", "lat", "lon"),
            P("lat", "lon"),
            P(),
            P(),
            P(),
        ),
        out_specs=(
            P("group", None, "lat", "lon"),
            P("group", "lat", "lon"),
            P("group", "lat", "lon"),
            P("group", "lat", "lon"),
        ),
        check_vma=False,
    )
```
